32 devices in a mesh: qa: 8 (over z, x), qb: 4 (over y, core).
Axes of the slice: x: 2, y: 2, z: 4, core: 2. Of those that a mesh axis runs over, the one named last changes fastest.
Arguments:
- state: float32 [8, 4, 128, 8, 128], P('qa', 'qb'), may hold values from -6 to 6
- costate: float32 [8, 4, 128, 8, 128], P('qa', 'qb'), may hold values from -6 to 6
- gates: float32 [2, 4, 128, 128], replicated, may hold values from -0.5 to 0.5
- targets: int32 [2, 4], replicated, may hold values from 0 to 1
Outputs:
- start_state: float32 [8, 4, 128, 8, 128], P('qa', 'qb')
- start_costate: float32 [8, 4, 128, 8, 128], P('qa', 'qb')
- gate_grads: float32 [2, 4, 128, 128], replicated
The draws below stay inside these ranges and needn't reach their ends.
Inputs may be any that keep to these rules, and one draw needn't show every extreme that they name: `targets`: 0 means the gate acts on the last index, 1 on the third from last.
All inputs are finite; a program needn't handle non-finite values.
Results may differ from the reference program's by a relative error of at most 0.0003.
Values sent between devices are 32-bit elements; how exact they have to be, the bound alone decides.
No kernel may reach another device: no remote copies, remote signals or barrier semaphores. Data moves between devices by JAX's collectives and lax.ppermute only.
A program may use at most 64 MiB of HBM per device.

```python
import jax
import jax.numpy as jnp
from jax import lax

GATE = 128
SLAB = 8
REST = 32768
N_QA = 8
N_QB = 4


def touch_ends(result, rng, least, largest):
    longest = result.shape.index(max(result.shape))
    spots = []
    for shift in (0, 1):
        where = [jax.random.randint(jax.random.fold_in(rng, axis), (), 0, length) for axis, length in enumerate(result.shape)]
        where[longest] = (where[longest] + shift) % result.shape[longest]
        spots.append(tuple(where))
    return result.at[spots[0]].set(least).at[spots[1]].set(largest)


def levels(key, dims, pieces, least, largest):
    loudness, own = 1.0, jax.random.fold_in(key, 6)
    for dim, parts in pieces:
        steps = jnp.exp(jax.random.uniform(jax.random.fold_in(own, dim), (parts,), jnp.float32, least / len(pieces), largest / len(pieces)))
        loudness = loudness * jnp.repeat(steps, dims[dim] // parts).reshape([-1 if axis == dim else 1 for axis in range(len(dims))])
    return loudness


def gaussian(rng, extent, deviation, most, cuts=(), kind=jnp.bfloat16):
    gain = levels(rng, extent, cuts, -0.22, 0.18) if cuts else 1.0
    values = jax.random.normal(rng, extent, jnp.float32) * deviation * gain
    return jnp.minimum(jnp.maximum(values, -most), most).astype(kind)


def setup_inputs(seed: int = 0) -> dict:
    key_list = jax.random.split(jax.random.key(seed), 5)
    return {
        "state": gaussian(key_list[0], (N_QA, N_QB, GATE, SLAB, GATE), 1.0, 6.0, ((0, 8), (1, 4)), jnp.float32),
        "costate": gaussian(key_list[1], (N_QA, N_QB, GATE, SLAB, GATE), 1.0, 6.0, ((0, 8), (1, 4)), jnp.float32),
        "gates": gaussian(key_list[2], (2, 4, GATE, GATE), GATE ** -0.5, 0.5, (), jnp.float32),
        "targets": touch_ends(jax.random.randint(key_list[3], (2, 4), 0, 2), jax.random.fold_in(key_list[3], 1), 0, 1).astype(jnp.int32),
    }


def unapply(values, matrix, target):
    def apply_low(inner):
        return jnp.einsum('abmsi,ij->abmsj', inner, matrix, precision=lax.Precision.HIGHEST)

    def apply_middle(inner):
        return jnp.einsum('abisl,ij->abjsl', inner, matrix, precision=lax.Precision.HIGHEST)

    return lax.cond(target == 0, apply_low, apply_middle, values)


def gradient(adjoint, earlier, target):
    def from_low(inner):
        return jnp.einsum('abmsi,abmsj->ij', inner[0], inner[1], precision=lax.Precision.HIGHEST)

    def from_middle(inner):
        return jnp.einsum('abisl,abjsl->ij', inner[0], inner[1], precision=lax.Precision.HIGHEST)

    return lax.cond(target == 0, from_low, from_middle, (adjoint, earlier))


def swap_qubits(values, position, count):
    layout = values.shape
    remain = layout[2] // count
    split_view = values.reshape(layout[0], layout[1], count, remain, layout[3], layout[4])
    return jnp.swapaxes(split_view, position, 2).reshape(layout)


def reference(state, costate, gates, targets):
    amplitudes = state
    adjoint = costate
    results = [None, None]
    for block_index in (1, 0):
        grad_list = []
        for gate_index in (3, 2, 1, 0):
            matrix = gates[block_index, gate_index]
            target = targets[block_index, gate_index]
            earlier = unapply(amplitudes, matrix, target)
            grad_list.append(gradient(adjoint, earlier, target))
            adjoint = unapply(adjoint, matrix, target)
            amplitudes = earlier
        results[block_index] = jnp.stack(grad_list[::-1])
        if block_index == 1:
            amplitudes = swap_qubits(amplitudes, 1, N_QB)
            adjoint = swap_qubits(adjoint, 1, N_QB)
        else:
            amplitudes = swap_qubits(amplitudes, 0, N_QA)
            adjoint = swap_qubits(adjoint, 0, N_QA)
    gate_grads = jnp.stack(results) * (REST ** -0.5)
    return amplitudes, adjoint, gate_grads
```

```python
import functools

import jax
import jax.numpy as jnp
from jax import lax
from jax.experimental import pallas as pl
from jax.experimental.pallas import tpu as pltpu
from jax.sharding import PartitionSpec as P

F32, BF16 = jnp.float32, jnp.bfloat16
VMEM_LIMIT = 32 * 1024 * 1024


def split(x):
    high = x.astype(BF16)
    return high, (x - high.astype(F32)).astype(BF16)


def dot(a, b, dims=((1,), (0,))):
    return lax.dot_general(a, b, (dims, ((), ())), preferred_element_type=F32)


def right_factor(u):
    high, low = split(u)
    row = jnp.concatenate([high, low], axis=1)
    return jnp.concatenate([row, row], axis=0)


def left_factor(u):
    high, low = split(jnp.transpose(u))
    return jnp.concatenate(
        [jnp.concatenate([high, high], axis=1), jnp.concatenate([low, low], axis=1)], axis=0
    )


def times_right(x, factor):
    d = x.shape[1]
    r = dot(jnp.concatenate(split(x), axis=1), factor)
    return r[:, :d] + r[:, d:]


def times_left(factor, x):
    d = x.shape[0]
    r = dot(factor, jnp.concatenate(split(x), axis=0))
    return r[:d] + r[d:]


def matmul(a, b):
    return times_right(a, right_factor(b))


def slab_of_native(ref, s):
    rows, slabs, lanes = ref.shape
    return ref.reshape(rows * slabs, lanes)[pl.ds(s, rows, stride=slabs), :]


def slab_of_parts(ref, a, s):
    n, _, _, r, lanes = ref.shape
    return ref[:, a, s].reshape(n * r, lanes)


def products(targets, gates, block):
    d = gates.shape[-1]
    eye = (
        lax.broadcasted_iota(jnp.int32, (d, d), 0) == lax.broadcasted_iota(jnp.int32, (d, d), 1)
    ).astype(F32)
    last = gates.shape[1] - 1
    u = gates[block, last]
    low_turn = targets[block, last] == 0
    low, mid = jnp.where(low_turn, u, eye), jnp.where(low_turn, eye, u)
    for g in range(last - 1, -1, -1):
        both = matmul(jnp.concatenate([low, mid], axis=0), gates[block, g])
        low_turn = targets[block, g] == 0
        low, mid = jnp.where(low_turn, both[:d], low), jnp.where(low_turn, mid, both[d:])
    return low, mid


def apply_kernel(block, native, targets, gates, *refs):
    out = refs[-1]
    n, _, slabs, r, d = out.shape
    low, mid = products(targets, gates, block)
    low, mid = right_factor(low), left_factor(mid)
    for s in range(slabs):
        if native:
            x, y = slab_of_native(refs[0], s), slab_of_native(refs[1], s)
        else:
            x, y = slab_of_parts(refs[0], 0, s), slab_of_parts(refs[0], 1, s)
        z = times_right(jnp.concatenate([x, y], axis=0), low)
        z = times_left(mid, jnp.concatenate([z[: n * r], z[n * r :]], axis=1))
        out[:, 0, s] = z[:, :d].reshape(n, r, d)
        out[:, 1, s] = z[:, d:].reshape(n, r, d)


def gradient_kernel(block, native, scale, targets, gates, *refs):
    out, held, inner = refs[-3:]
    slabs, d = held.shape[1], held.shape[3]
    for s in range(slabs):
        for a in range(2):
            held[a, s] = slab_of_native(refs[a], s) if native else slab_of_parts(refs[0], a, s)

    def contract_low():
        total = jnp.zeros((2 * d, 2 * d), F32)
        for s in range(slabs):
            y = jnp.concatenate(split(held[1, s]), axis=1)
            x = jnp.concatenate(split(held[0, s]), axis=1)
            total = total + dot(y, x, ((0,), (0,)))
        inner[...] = (total[:d, :d] + total[d:, d:]) + (total[:d, d:] + total[d:, :d])

    def contract_mid():
        total = jnp.zeros((2 * d, 2 * d), F32)
        for s in range(slabs):
            y = jnp.concatenate(split(held[1, s]), axis=0)
            x = jnp.concatenate(split(held[0, s]), axis=0)
            total = total + dot(y, x, ((1,), (1,)))
        inner[...] = (total[:d, :d] + total[d:, d:]) + (total[:d, d:] + total[d:, :d])

    def apply_low(u):
        factor = right_factor(u)
        for s in range(slabs):
            z = times_right(jnp.concatenate([held[0, s], held[1, s]], axis=0), factor)
            held[0, s], held[1, s] = z[:d], z[d:]

    def apply_mid(u):
        factor = left_factor(u)
        for s in range(slabs):
            z = times_left(factor, jnp.concatenate([held[0, s], held[1, s]], axis=1))
            held[0, s], held[1, s] = z[:, :d], z[:, d:]

    last = gates.shape[1] - 1
    pending = None
    for g in range(last, -1, -1):
        low_turn = targets[block, g] == 0
        fresh = True if g == last else targets[block, g] != targets[block, g + 1]
        pl.when(jnp.logical_and(fresh, low_turn))(contract_low)
        pl.when(jnp.logical_and(fresh, jnp.logical_not(low_turn)))(contract_mid)
        u = gates[block, g]
        grad = matmul(inner[...], u)
        out[g] = grad * scale
        if g == 0:
            break
        inner[...] = times_left(left_factor(u), grad)
        pending = u if g == last else jnp.where(fresh, u, matmul(pending, u))
        turn = targets[block, g - 1] != targets[block, g]
        pl.when(jnp.logical_and(turn, low_turn))(lambda p=pending: apply_low(p))
        pl.when(jnp.logical_and(turn, jnp.logical_not(low_turn)))(lambda p=pending: apply_mid(p))


def store_kernel(parts, first, second):
    n, _, slabs, r, d = parts.shape
    for a, out in enumerate((first, second)):
        flat = out.reshape(n * r * slabs, d)
        for s in range(slabs):
            flat[pl.ds(s, n * r, stride=slabs), :] = slab_of_parts(parts, a, s)


def call(kernel, out_shape, inputs, scratch=(), flops=0):
    specs = [
        pl.BlockSpec(memory_space=pltpu.SMEM if x.dtype == jnp.int32 else pltpu.VMEM)
        for x in inputs
    ]
    outs = jax.tree.map(lambda _: pl.BlockSpec(memory_space=pltpu.VMEM), out_shape)
    size = sum(x.size * 4 for x in inputs) + sum(x.size * 4 for x in jax.tree.leaves(out_shape))
    return pl.pallas_call(
        kernel,
        out_shape=out_shape,
        in_specs=specs,
        out_specs=outs,
        scratch_shapes=list(scratch),
        compiler_params=pltpu.CompilerParams(vmem_limit_bytes=VMEM_LIMIT),
        cost_estimate=pl.CostEstimate(flops=flops, bytes_accessed=size, transcendentals=0),
    )(*inputs)


def shards(state, costate, gates, targets):
    layout = state.shape
    rows, slabs, d = layout[2:]
    n_qa, n_qb = lax.axis_size("qa"), lax.axis_size("qb")
    scale = (n_qa * n_qb * rows * slabs) ** -0.5
    natives = [state.reshape(layout[2:]), costate.reshape(layout[2:])]
    parts_qb = jax.ShapeDtypeStruct((n_qb, 2, slabs, rows // n_qb, d), F32)
    parts_qa = jax.ShapeDtypeStruct((n_qa, 2, slabs, rows // n_qa, d), F32)
    grads = jax.ShapeDtypeStruct(gates.shape[1:], F32)
    scratch = [pltpu.VMEM((2, slabs, rows, d), F32), pltpu.VMEM((d, d), F32)]
    work = 2 * 2 * 2 * 4 * rows * slabs * d * d

    sent = call(functools.partial(apply_kernel, 1, True), parts_qb, [targets, gates, *natives], flops=work)
    parts = lax.all_to_all(sent, "qb", 0, 0, tiled=True)
    grads1 = call(
        functools.partial(gradient_kernel, 1, True, scale), grads, [targets, gates, *natives], scratch, 8 * work
    )
    sent = call(functools.partial(apply_kernel, 0, False), parts_qa, [targets, gates, parts], flops=work)
    last = lax.all_to_all(sent, "qa", 0, 0, tiled=True)
    grads0 = call(
        functools.partial(gradient_kernel, 0, False, scale), grads, [targets, gates, parts], scratch, 8 * work
    )
    both = jnp.stack([grads0, grads1])
    shares = both.reshape(n_qa * n_qb, -1, d)
    share = lax.all_to_all(shares, ("qa", "qb"), 0, 0, tiled=True).sum(0, keepdims=True)
    whole = lax.all_to_all(jnp.broadcast_to(share, shares.shape), ("qa", "qb"), 0, 0, tiled=True)
    native = jax.ShapeDtypeStruct(layout[2:], F32)
    first, second = call(store_kernel, (native, native), [last])
    return first.reshape(layout), second.reshape(layout), whole.reshape(gates.shape)


def solution(mesh):
    in_specs = (P("qa", "qb", None, None, None), P("qa", "qb", None, None, None), P(), P())
    out_specs = (P("qa", "qb", None, None, None), P("qa", "qb", None, None, None), P())
    return jax.shard_map(shards, mesh=mesh, in_specs=in_specs, out_specs=out_specs, check_vma=False)
```

```python
import functools

import jax
import jax.numpy as jnp
from jax import lax
from jax.experimental import pallas as pl
from jax.experimental.pallas import tpu as pltpu
from jax.sharding import PartitionSpec as P

F32, BF16 = jnp.float32, jnp.bfloat16
VMEM_LIMIT = 32 * 1024 * 1024


def split(x):
    high = x.astype(BF16)
    return high, (x - high.astype(F32)).astype(BF16)


def dot(a, b, dims=((1,), (0,))):
    return lax.dot_general(a, b, (dims, ((), ())), preferred_element_type=F32)


def right_factor(u):
    high, low = split(u)
    row = jnp.concatenate([high, low], axis=1)
    return jnp.concatenate([row, row], axis=0)


def left_factor(u):
    return stack_factor(jnp.transpose(u))


def stack_factor(u):
    high, low = split(u)
    return jnp.concatenate(
        [jnp.concatenate([high, high], axis=1), jnp.concatenate([low, low], axis=1)], axis=0
    )


def times_right(x, factor):
    d = x.shape[1]
    r = dot(jnp.concatenate(split(x), axis=1), factor)
    return r[:, :d] + r[:, d:]


def times_left(factor, x):
    d = x.shape[0]
    r = dot(factor, jnp.concatenate(split(x), axis=0))
    return r[:d] + r[d:]


def matmul(a, b):
    return times_right(a, right_factor(b))


def slab_of_native(ref, s):
    rows, slabs, lanes = ref.shape
    return ref.reshape(rows * slabs, lanes)[pl.ds(s, rows, stride=slabs), :]


def slab_of_parts(ref, a, s):
    n, _, _, r, lanes = ref.shape
    return ref[:, a, s].reshape(n * r, lanes)


def products(targets, gates, block, at):
    d = gates.shape[-1]
    eye = (
        lax.broadcasted_iota(jnp.int32, (d, d), 0) == lax.broadcasted_iota(jnp.int32, (d, d), 1)
    ).astype(F32)
    last = gates.shape[1] - 1
    u = gates[at, last]
    low_turn = targets[block, last] == 0
    low, mid = jnp.where(low_turn, u, eye), jnp.where(low_turn, eye, u)
    for g in range(last - 1, -1, -1):
        both = matmul(jnp.concatenate([low, mid], axis=0), gates[at, g])
        low_turn = targets[block, g] == 0
        low, mid = jnp.where(low_turn, both[:d], low), jnp.where(low_turn, mid, both[d:])
    return low, mid


def apply_kernel(block, native, targets, gates, *refs):
    out = refs[-1]
    n, _, slabs, r, d = out.shape
    low, mid = products(targets, gates, block, block)
    low, mid = right_factor(low), left_factor(mid)
    for s in range(slabs):
        if native:
            x, y = slab_of_native(refs[0], s), slab_of_native(refs[1], s)
        else:
            x, y = slab_of_parts(refs[0], 0, s), slab_of_parts(refs[0], 1, s)
        z = times_right(jnp.concatenate([x, y], axis=0), low)
        z = times_left(mid, jnp.concatenate([z[: n * r], z[n * r :]], axis=1))
        out[:, 0, s] = z[:, :d].reshape(n, r, d)
        out[:, 1, s] = z[:, d:].reshape(n, r, d)


def block_kernel(block, load, store, emit, scale, targets, gates, held, inner, grads):
    slabs, d = held.shape[1], held.shape[3]
    load(held)

    def contract_low():
        total = jnp.zeros((2 * d, 2 * d), F32)
        for s in range(slabs):
            y = jnp.concatenate(split(held[1, s]), axis=1)
            x = jnp.concatenate(split(held[0, s]), axis=1)
            total = total + dot(y, x, ((0,), (0,)))
        inner[...] = (total[:d, :d] + total[d:, d:]) + (total[:d, d:] + total[d:, :d])

    def contract_mid():
        total = jnp.zeros((2 * d, 2 * d), F32)
        for s in range(slabs):
            y = jnp.concatenate(split(held[1, s]), axis=0)
            x = jnp.concatenate(split(held[0, s]), axis=0)
            total = total + dot(y, x, ((1,), (1,)))
        inner[...] = (total[:d, :d] + total[d:, d:]) + (total[:d, d:] + total[d:, :d])

    def put(s, x, y):
        held[0, s], held[1, s] = x, y

    def apply_low(u, put):
        factor = right_factor(u)
        for s in range(slabs):
            z = times_right(jnp.concatenate([held[0, s], held[1, s]], axis=0), factor)
            put(s, z[:d], z[d:])

    def apply_mid(u, put):
        factor = left_factor(u)
        for s in range(slabs):
            z = times_left(factor, jnp.concatenate([held[0, s], held[1, s]], axis=1))
            put(s, z[:, :d], z[:, d:])

    last = gates.shape[1] - 1
    pending = None
    for g in range(last, -1, -1):
        low_turn = targets[block, g] == 0
        fresh = True if g == last else targets[block, g] != targets[block, g + 1]
        pl.when(jnp.logical_and(fresh, low_turn))(contract_low)
        pl.when(jnp.logical_and(fresh, jnp.logical_not(low_turn)))(contract_mid)
        u = gates[block, g]
        grad = matmul(inner[...], u)
        grads[g] = grad * scale
        pending = u if g == last else jnp.where(fresh, u, matmul(pending, u))
        if g == 0:
            break
        inner[...] = times_left(left_factor(u), grad)
        turn = targets[block, g - 1] != targets[block, g]
        pl.when(jnp.logical_and(turn, low_turn))(lambda p=pending: apply_low(p, put))
        pl.when(jnp.logical_and(turn, jnp.logical_not(low_turn)))(lambda p=pending: apply_mid(p, put))
    if store is not None:
        pl.when(low_turn)(lambda: apply_low(pending, store))
        pl.when(jnp.logical_not(low_turn))(lambda: apply_mid(pending, store))
    emit(grads)


def gradient_kernel(block, scale, targets, gates, *refs):
    out, held, inner = refs[-3:]

    def load(held):
        for s in range(held.shape[1]):
            for a in range(2):
                held[a, s] = slab_of_native(refs[a], s)

    block_kernel(block, load, None, lambda grads: None, scale, targets, gates, held, inner, out)


def slabs_gradient_kernel(block, scale, targets, gates, parts, out, held, inner):
    def load(held):
        for s in range(held.shape[1]):
            for a in range(2):
                held[a, s] = slab_of_parts(parts, a, s)

    block_kernel(block, load, None, lambda grads: None, scale, targets, gates, held, inner, out)


def second_kernel(block, n_qb, scale, targets, gates, *refs):
    blocks, (out, keep, send, held, inner, grads) = refs[:n_qb], refs[n_qb:]
    n, _, slabs, r, d = out.shape
    mine = lax.axis_index("qb")

    def load(held):
        for k, ref in enumerate(blocks):
            count = ref.shape[2]
            rows = pl.ds(pl.multiple_of((mine ^ k) * count, count), count)
            held[:, :, rows] = ref[...]

    def store(s, x, y):
        out[:, 0, s] = x.reshape(n, r, d)
        out[:, 1, s] = y.reshape(n, r, d)

    def emit(grads):
        half = grads.shape[0] // 2
        core = mine % 2
        keep[...] = grads[pl.ds(core * half, half)].reshape(keep.shape)
        send[...] = grads[pl.ds((1 - core) * half, half)].reshape(send.shape)

    block_kernel(block, load, store, emit, scale, targets, gates, held, inner, grads)


def first_kernel(block, n_qb, targets, gates, state, costate, *refs):
    outs, (mats, x_ref, y_ref, turned, sems) = refs[:n_qb], refs[n_qb:]
    copies = [
        pltpu.make_async_copy(gates.at[pl.ds(block, 1)], mats, sems.at[0]),
        pltpu.make_async_copy(state, x_ref, sems.at[1]),
        pltpu.make_async_copy(costate, y_ref, sems.at[2]),
    ]
    for copy in copies:
        copy.start()
    _, slabs, r, d = outs[0].shape
    mine = lax.axis_index("qb")
    copies[0].wait()
    low, mid = products(targets, mats, block, 0)
    low = right_factor(low)
    turned[...] = jnp.transpose(mid)
    mid = jnp.concatenate(
        [turned[pl.ds(pl.multiple_of((mine ^ k) * r, r), r), :] for k in range(n_qb)], axis=0
    )
    mid = stack_factor(mid)
    copies[1].wait()
    copies[2].wait()
    for s in range(slabs):
        x, y = slab_of_native(x_ref, s), slab_of_native(y_ref, s)
        z = times_right(jnp.concatenate([x, y], axis=0), low)
        z = times_left(mid, jnp.concatenate([z[:d], z[d:]], axis=1))
        for k, out in enumerate(outs):
            out[0, s] = z[k * r : (k + 1) * r, :d]
            out[1, s] = z[k * r : (k + 1) * r, d:]


def halve_kernel(parts, keep, send, total):
    total[...] = functools.reduce(lambda a, b: a + b, [parts[i] for i in range(parts.shape[0])])
    core = lax.axis_index("qb") % 2
    half = keep.shape[0]
    keep[...] = total[pl.ds(pl.multiple_of(core * half, half), half), :]
    send[...] = total[pl.ds(pl.multiple_of((1 - core) * half, half), half), :]


def plane_partners(n_qb):
    return [(dx, dy) for dx in range(2) for dy in range(n_qb // 2)]


def share_kernel(n_qb, keep0, got0, keep1, got1, *refs):
    outs, (sum0, sum1) = refs[:-2], refs[-2:]
    sum0[...] = keep0[...] + got0[...]
    sum1[...] = keep1[...] + got1[...]
    x, y = lax.axis_index("qa") % 2, lax.axis_index("qb") // 2
    size0, size1 = sum0.shape[0] // n_qb, sum1.shape[0] // (n_qb // 2)
    for (dx, dy), out in zip(plane_partners(n_qb), outs):
        place = (x ^ dx) * (n_qb // 2) + (y ^ dy)
        out[:size0] = sum0[pl.ds(pl.multiple_of(place * size0, size0), size0), :]
        if dx == 0:
            out[size0:] = sum1[pl.ds(pl.multiple_of((y ^ dy) * size1, size1), size1), :]


def plane_sum_kernel(n_qb, *refs):
    ins, out = refs[:-1], refs[-1]
    size0 = ins[-1].shape[0]
    out[:size0] = functools.reduce(lambda a, b: a + b, [ref[:size0] for ref in ins])
    out[size0:] = functools.reduce(lambda a, b: a + b, [ref[size0:] for ref in ins[: n_qb // 2]])


def line_sum_kernel(size0, *refs):
    ins, out, held = refs[:-2], refs[-2], refs[-1]
    line = lax.axis_index("qa") // 2
    size1 = ins[0].shape[0] - size0
    for k, ref in enumerate(ins):
        held[line ^ k] = ref[:size0]
        out[pl.ds(size0 + k * size1, size1), :] = ref[size0:]
    out[:size0] = functools.reduce(lambda a, b: a + b, [held[i] for i in range(len(ins))])


def collect_kernel(n_qa, n_qb, size0, *refs):
    ins, out = refs[:-1], refs[-1]
    rows = out.shape[1]
    size1 = rows // (n_qa * n_qb)
    a, b = lax.axis_index("qa"), lax.axis_index("qb")
    for i, ref in enumerate(ins):
        dc, (dx, dy) = i // n_qb, plane_partners(n_qb)[i % n_qb]
        x, y, core = (a % 2) ^ dx, (b // 2) ^ dy, (b % 2) ^ dc
        row = core * (rows // 2) + (x * (n_qb // 2) + y) * size0
        out[0, pl.ds(pl.multiple_of(row, size0), size0), :] = ref[:size0]
        for dz in range(n_qa // 2):
            row = ((((a // 2) ^ dz) * 2 + x) * 2 + core) * (n_qb // 2) + y
            row = pl.multiple_of(row * size1, size1)
            out[1, pl.ds(row, size1), :] = ref[size0 + dz * size1 : size0 + (dz + 1) * size1]


def store_kernel(parts, first, second):
    n, _, slabs, r, d = parts.shape
    for a, out in enumerate((first, second)):
        flat = out.reshape(n * r * slabs, d)
        for s in range(slabs):
            flat[pl.ds(s, n * r, stride=slabs), :] = slab_of_parts(parts, a, s)


def call(kernel, out_shape, inputs, scratch=(), flops=0, far=()):
    def spec(i, x):
        if x.dtype == jnp.int32:
            return pl.BlockSpec(memory_space=pltpu.SMEM)
        return pl.BlockSpec(memory_space=pl.ANY if i in far else pltpu.VMEM)

    outs = jax.tree.map(lambda _: pl.BlockSpec(memory_space=pltpu.VMEM), out_shape)
    size = sum(x.size * 4 for x in inputs) + sum(x.size * 4 for x in jax.tree.leaves(out_shape))
    return pl.pallas_call(
        kernel,
        out_shape=out_shape,
        in_specs=[spec(i, x) for i, x in enumerate(inputs)],
        out_specs=outs,
        scratch_shapes=list(scratch),
        compiler_params=pltpu.CompilerParams(vmem_limit_bytes=VMEM_LIMIT),
        cost_estimate=pl.CostEstimate(flops=flops, bytes_accessed=size, transcendentals=0),
    )(*inputs)


def shape(*dims):
    return jax.ShapeDtypeStruct(dims, F32)


def exchange(x, da, db):
    n_qa, n_qb = lax.axis_size("qa"), lax.axis_size("qb")
    pairs = [(a * n_qb + b, (a ^ da) * n_qb + (b ^ db)) for a in range(n_qa) for b in range(n_qb)]
    return lax.ppermute(x, ("qa", "qb"), pairs)


def summed(grads0, grads1):
    both = jnp.stack([grads0, grads1])
    shares = both.reshape(lax.axis_size("qa") * lax.axis_size("qb"), -1, both.shape[-1])
    share = lax.all_to_all(shares, ("qa", "qb"), 0, 0, tiled=True).sum(0, keepdims=True)
    return lax.all_to_all(jnp.broadcast_to(share, shares.shape), ("qa", "qb"), 0, 0, tiled=True)


def shards(state, costate, gates, targets):
    layout = state.shape
    rows, slabs, d = layout[2:]
    n_qa, n_qb = lax.axis_size("qa"), lax.axis_size("qb")
    scale = (n_qa * n_qb * rows * slabs) ** -0.5
    native = shape(*layout[2:])
    natives = [state.reshape(native.shape), costate.reshape(native.shape)]
    r = rows // n_qb
    parts_qa = shape(n_qa, 2, slabs, rows // n_qa, d)
    held, square = pltpu.VMEM((2, slabs, rows, d), F32), pltpu.VMEM((d, d), F32)
    work = 2 * 2 * 2 * 4 * rows * slabs * d * d
    count = gates.shape[1]
    every = count * d

    if every % (8 * n_qa * n_qb) or r % 8 or n_qa % 2 or n_qb % 2:
        parts_qb = shape(n_qb, 2, slabs, r, d)
        sent = call(functools.partial(apply_kernel, 1, True), parts_qb, [targets, gates, *natives], flops=work)
        parts = lax.all_to_all(sent, "qb", 0, 0, tiled=True)
        grads1 = call(
            functools.partial(gradient_kernel, 1, scale),
            shape(count, d, d), [targets, gates, *natives], [held, square], 8 * work,
        )
        sent = call(functools.partial(apply_kernel, 0, False), parts_qa, [targets, gates, parts], flops=work)
        last = lax.all_to_all(sent, "qa", 0, 0, tiled=True)
        grads0 = call(
            functools.partial(slabs_gradient_kernel, 0, scale),
            shape(count, d, d), [targets, gates, parts], [held, square], 8 * work,
        )
        whole = summed(grads0, grads1)
    else:
        blocks = call(
            functools.partial(first_kernel, 1, n_qb),
            [shape(2, slabs, r, d)] * n_qb,
            [targets, gates, *natives],
            [
                pltpu.VMEM((1, *gates.shape[1:]), F32),
                pltpu.VMEM(native.shape, F32),
                pltpu.VMEM(native.shape, F32),
                square,
                pltpu.SemaphoreType.DMA((3,)),
            ],
            work,
            far=(1, 2, 3),
        )
        blocks = [blocks[0]] + [exchange(blocks[k], 0, k) for k in range(1, n_qb)]
        grads1 = call(
            functools.partial(gradient_kernel, 1, scale),
            shape(count, d, d), [targets, gates, *natives], [held, square], 4 * work,
        )
        part1 = lax.all_to_all(grads1.reshape(n_qa, -1, d), "qa", 0, 0, tiled=True)

        half = shape(every // 2, d)
        sent, keep0, send0 = call(
            functools.partial(second_kernel, 0, n_qb, scale),
            (parts_qa, half, half),
            [targets, gates, *blocks],
            [held, square, pltpu.VMEM((count, d, d), F32)],
            6 * work,
        )
        last = lax.all_to_all(sent, "qa", 0, 0, tiled=True)

        whole1 = every // n_qa
        keep1, send1 = call(
            halve_kernel, (shape(whole1 // 2, d),) * 2, [part1], [pltpu.VMEM((whole1, d), F32)]
        )
        size0, size1 = every // 2 // n_qb, every // (n_qa * n_qb)
        partners = plane_partners(n_qb)
        shares = call(
            functools.partial(share_kernel, n_qb),
            [shape(size0 + (size1 if dx == 0 else 0), d) for dx, _ in partners],
            [keep0, exchange(send0, 0, 1), keep1, exchange(send1, 0, 1)],
            [pltpu.VMEM(half.shape, F32), pltpu.VMEM((whole1 // 2, d), F32)],
        )
        shares = [shares[0]] + [exchange(x, dx, 2 * dy) for x, (dx, dy) in zip(shares[1:], partners[1:])]
        mine = call(functools.partial(plane_sum_kernel, n_qb), shape(size0 + size1, d), shares)
        lines = [mine] + [exchange(mine, 2 * dz, 0) for dz in range(1, n_qa // 2)]
        mine = call(
            functools.partial(line_sum_kernel, size0),
            shape(size0 + size1 * (n_qa // 2), d),
            lines,
            [pltpu.VMEM((n_qa // 2, size0, d), F32)],
        )
        found = [mine] + [exchange(mine, dx, 2 * dy) for dx, dy in partners[1:]]
        found = found + [exchange(x, 0, 1) for x in found]
        whole = call(
            functools.partial(collect_kernel, n_qa, n_qb, size0), shape(gates.shape[0], every, d), found
        )
    first, second = call(store_kernel, (native, native), [last])
    return first.reshape(layout), second.reshape(layout), whole.reshape(gates.shape)


def solution(mesh):
    in_specs = (P("qa", "qb", None, None, None), P("qa", "qb", None, None, None), P(), P())
    out_specs = (P("qa", "qb", None, None, None), P("qa", "qb", None, None, None), P())
    return jax.shard_map(shards, mesh=mesh, in_specs=in_specs, out_specs=out_specs, check_vma=False)
```

```python
import functools

import jax
import jax.numpy as jnp
from jax import lax
from jax.experimental import pallas as pl
from jax.experimental.pallas import tpu as pltpu
from jax.sharding import PartitionSpec as P

F32, BF16 = jnp.float32, jnp.bfloat16
K0COST = 50
PARTS_DUE = 'plane'
WINDOWS = [(0, 'plane'), (1, ('line', 1)), (1, ('line', 2)), ('plane', ('back', 0)), (('line', 1), ('back', 1)), (0, ('line', 1)), (1, ('line', 2))]
VMEM_LIMIT = 16 * 1024 * 1024


def split(x):
    high = x.astype(BF16)
    return high, (x - high.astype(F32)).astype(BF16)


def dot(a, b, dims=((1,), (0,))):
    return lax.dot_general(a, b, (dims, ((), ())), preferred_element_type=F32)


def right_factor(u):
    high, low = split(u)
    row = jnp.concatenate([high, low], axis=1)
    return jnp.concatenate([row, row], axis=0)


def left_factor(u):
    return stack_factor(jnp.transpose(u))


def stack_factor(u):
    high, low = split(u)
    return jnp.concatenate(
        [jnp.concatenate([high, high], axis=1), jnp.concatenate([low, low], axis=1)], axis=0
    )


def times_right(x, factor):
    d = x.shape[1]
    r = dot(jnp.concatenate(split(x), axis=1), factor)
    return r[:, :d] + r[:, d:]


def times_left(factor, x):
    d = x.shape[0]
    r = dot(factor, jnp.concatenate(split(x), axis=0))
    return r[:d] + r[d:]


def matmul(a, b):
    return times_right(a, right_factor(b))


def slab_of_native(ref, s):
    rows, slabs, lanes = ref.shape
    return ref.reshape(rows * slabs, lanes)[pl.ds(s, rows, stride=slabs), :]


def slab_of_parts(ref, a, s):
    n, _, _, r, lanes = ref.shape
    return ref[:, a, s].reshape(n * r, lanes)


def products(targets, gates, block, at):
    d = gates.shape[-1]
    eye = (
        lax.broadcasted_iota(jnp.int32, (d, d), 0) == lax.broadcasted_iota(jnp.int32, (d, d), 1)
    ).astype(F32)
    last = gates.shape[1] - 1
    u = gates[at, last]
    low_turn = targets[block, last] == 0
    low, mid = jnp.where(low_turn, u, eye), jnp.where(low_turn, eye, u)
    for g in range(last - 1, -1, -1):
        both = matmul(jnp.concatenate([low, mid], axis=0), gates[at, g])
        low_turn = targets[block, g] == 0
        low, mid = jnp.where(low_turn, both[:d], low), jnp.where(low_turn, mid, both[d:])
    return low, mid


def apply_kernel(block, native, targets, gates, *refs):
    out = refs[-1]
    n, _, slabs, r, d = out.shape
    low, mid = products(targets, gates, block, block)
    low, mid = right_factor(low), left_factor(mid)
    for s in range(slabs):
        if native:
            x, y = slab_of_native(refs[0], s), slab_of_native(refs[1], s)
        else:
            x, y = slab_of_parts(refs[0], 0, s), slab_of_parts(refs[0], 1, s)
        z = times_right(jnp.concatenate([x, y], axis=0), low)
        z = times_left(mid, jnp.concatenate([z[: n * r], z[n * r :]], axis=1))
        out[:, 0, s] = z[:, :d].reshape(n, r, d)
        out[:, 1, s] = z[:, d:].reshape(n, r, d)


def fuse(x):
    return jnp.concatenate(split(x), axis=-1)


def stacked(x):
    d = x.shape[-1] // 2
    return jnp.concatenate([x[:, :d], x[:, d:]], axis=0)


def same_run(targets, block, g):
    return targets[block, g] == targets[block, g + 1]


def identity(d):
    rows, columns = (lax.broadcasted_iota(jnp.int32, (d, d), i) for i in range(2))
    return (rows == columns).astype(F32)


def chains(targets, gates, right, left, made, kept):
    blocks, count, d, _ = gates.shape
    eye = identity(d)
    for block in range(blocks):
        left[block, count] = left_factor(eye)
        made[block] = eye
    made[blocks] = eye
    made[blocks + 1] = eye

    def step(i, _):
        g = count - 1 - i
        for block in range(blocks):
            u = gates[block, g]
            after = jnp.minimum(g + 1, count - 1)
            going = jnp.logical_and(i > 0, targets[block, g] == targets[block, after])
            p = jnp.where(going, matmul(made[block], u), u)
            made[block] = p
            if block:
                right[block, g] = right_factor(p)
                left[block, g] = left_factor(p)
            else:
                kept[g] = p
        both = made[pl.ds(blocks, 2)].reshape(2 * d, d)
        both = matmul(both, gates[0, g])
        low_turn = targets[0, g] == 0
        made[blocks] = jnp.where(low_turn, both[:d], made[blocks])
        made[blocks + 1] = jnp.where(low_turn, made[blocks + 1], both[d:])
        return _

    lax.fori_loop(0, count, step, 0)


def block_kernel(block, at, finish_from, scale, targets, right, left, held, inner, grads, ready=None):
    _, slabs, rows, d = held.shape
    d = d // 2
    count = grads.shape[0]

    def contract_low():
        y, x = (held[a].reshape(slabs * rows, 2 * d) for a in (1, 0))
        return dot(y, x, ((0,), (0,)))

    def contract_mid():
        y, x = (
            jnp.concatenate([stacked(held[a, s]) for s in range(slabs)], axis=1) for a in (1, 0)
        )
        return dot(y, x, ((1,), (1,)))

    def contract(g, how):
        total = how()
        inner[g] = (total[:d, :d] + total[d:, d:]) + (total[:d, d:] + total[d:, :d])

    def apply_low(g, begin=0):
        step = slabs // 2
        for a in range(2):
            for s in range(begin, slabs, step):
                r = dot(held[a, pl.ds(s, step)].reshape(step * rows, 2 * d), right[at, g])
                held[a, pl.ds(s, step)] = fuse((r[:, :d] + r[:, d:]).reshape(step, rows, d))

    def apply_mid(g, begin=0):
        for s in range(begin, slabs, 2):
            pairs = [(a, s + j) for a in range(2) for j in range(2)]
            x = jnp.concatenate([stacked(held[pair]) for pair in pairs], axis=1)
            r = dot(left[at, g], x)
            r = r[:d] + r[d:]
            for j, pair in enumerate(pairs):
                held[pair] = fuse(r[:, j * d : (j + 1) * d])

    def step(i, _):
        g = count - 1 - i
        low_turn = targets[block, g] == 0
        mid_turn = jnp.logical_not(low_turn)
        fresh = jnp.logical_or(i == 0, targets[block, g] != targets[block, jnp.minimum(g + 1, count - 1)])
        pl.when(jnp.logical_and(fresh, low_turn))(lambda: contract(g, contract_low))
        pl.when(jnp.logical_and(fresh, mid_turn))(lambda: contract(g, contract_mid))
        if ready is not None:
            pl.when(i == 0)(ready)
        turn = targets[block, g] != targets[block, jnp.maximum(g - 1, 0)]
        pl.when(jnp.logical_and(turn, low_turn))(lambda: apply_low(g))
        pl.when(jnp.logical_and(turn, mid_turn))(lambda: apply_mid(g))
        return _

    lax.fori_loop(0, count, step, 0)
    if finish_from < slabs:
        low_turn = targets[block, 0] == 0
        pl.when(low_turn)(lambda: apply_low(0, finish_from))
        pl.when(jnp.logical_not(low_turn))(lambda: apply_mid(0, finish_from))
    first = [count - 1] * count
    before = [count] * count
    for g in range(count - 2, -1, -1):
        going = same_run(targets, block, g)
        first[g] = jnp.where(going, first[g + 1], g)
        before[g] = jnp.where(going, g + 1, count)
    moved = [times_right(inner[first[g]], right[at, g]) for g in range(count)]
    for g in range(count):
        grads[g] = times_left(left[at, before[g]], moved[g]) * scale


def halves(grads, keep, send):
    half = grads.shape[0] // 2
    core = lax.axis_index("qb") % 2
    keep[...] = grads[pl.ds(core * half, half)].reshape(keep.shape)
    send[...] = grads[pl.ds((1 - core) * half, half)].reshape(send.shape)


def first_gradient_kernel(block, scale, *refs):
    refs, (keep, send, far0, low0, mid0, held, inner, right, left, made, grads, near0, sem) = refs[:4], refs[4:]
    gradient_kernel(block, scale, *refs, grads, near0, held, inner, right, left, made)
    copy = pltpu.make_async_copy(near0, far0, sem)
    copy.start()
    low0[...] = right_factor(made[made.shape[0] - 2])
    mid0[...] = left_factor(made[made.shape[0] - 1])
    halves(grads, keep, send)
    copy.wait()


def build(products, right, left):
    count, d, _ = products.shape
    for g in range(count):
        right[0, g] = right_factor(products[g])
        left[0, g] = left_factor(products[g])
    left[0, count] = left_factor(identity(d))


def gradient_kernel(block, scale, targets, gates, state, costate, out, factors0, held, inner, right, left, made):
    chains(targets, gates, right, left, made, factors0)
    for s in range(held.shape[1]):
        for a, ref in enumerate((state, costate)):
            held[a, s] = fuse(slab_of_native(ref, s))
    block_kernel(block, block, held.shape[1], scale, targets, right, left, held, inner, out)


def slabs_gradient_kernel(block, scale, targets, products, parts, out, held, inner, right, left):
    build(products, right, left)
    for s in range(held.shape[1]):
        for a in range(2):
            held[a, s] = fuse(slab_of_parts(parts, a, s))
    block_kernel(block, 0, held.shape[1], scale, targets, right, left, held, inner, out)


def early_kernel(n_qb, low, mid, *refs):
    blocks, (out, held) = refs[:n_qb], refs[n_qb:]
    n, _, slabs, r, d = out.shape
    gather(blocks, lambda rows, x: held.__setitem__((slice(None), slice(None), rows), x))
    for s in range(slabs):
        z = times_right(jnp.concatenate([held[0, s], held[1, s]], axis=0), low[...])
        z = times_left(mid[...], jnp.concatenate([z[: n * r], z[n * r :]], axis=1))
        for a in range(2):
            out[:, a, s] = z[:, a * d : (a + 1) * d].reshape(n, r, d)


def gather(blocks, put):
    mine = lax.axis_index("qb")
    for k, ref in enumerate(blocks):
        count = ref.shape[2]
        put(pl.ds(pl.multiple_of((mine ^ k) * count, count), count), ref[...])


def second_kernel(block, n_qa, n_qb, early, scale, targets, products, *refs):
    blocks, outs = (refs[:n_qb], refs[n_qb : 2 * n_qb]), refs[2 * n_qb : 2 * n_qb + n_qa]
    keep, send, held, inner, grads, here, right, left, sem = refs[2 * n_qb + n_qa :]
    copy = pltpu.make_async_copy(products, here, sem)
    copy.start()

    def ready():
        copy.wait()
        build(here, right, left)

    d = inner.shape[-1]
    for slabs, part in zip((slice(0, early), slice(early, None)), blocks):
        gather(part, lambda rows, x: held.__setitem__((slice(None), slabs, rows), fuse(x)))
    block_kernel(block, 0, early, scale, targets, right, left, held, inner, grads, ready)
    for k, ref in enumerate(outs):
        count = ref.shape[2]
        rows = pl.ds(pl.multiple_of((lax.axis_index("qa") ^ k) * count, count), count)
        part = held[:, early:, rows].astype(F32)
        ref[...] = part[..., :d] + part[..., d:]
    halves(grads, keep, send)


def first_kernel(block, n_qb, far_targets, gates, state, costate, *refs):
    outs, (targets, mats, x_ref, y_ref, turned, sems) = refs[: 2 * n_qb], refs[2 * n_qb :]
    copies = [
        pltpu.make_async_copy(far_targets, targets, sems.at[3]),
        pltpu.make_async_copy(gates.at[pl.ds(block, 1)], mats, sems.at[0]),
        pltpu.make_async_copy(state, x_ref, sems.at[1]),
        pltpu.make_async_copy(costate, y_ref, sems.at[2]),
    ]
    for copy in copies:
        copy.start()
    slabs = x_ref.shape[1]
    _, early, r, d = outs[0].shape
    mine = lax.axis_index("qb")
    copies[0].wait()
    copies[1].wait()
    low, mid = products(targets, mats, block, 0)
    low = right_factor(low)
    turned[...] = jnp.transpose(mid)
    mid = jnp.concatenate(
        [turned[pl.ds(pl.multiple_of((mine ^ k) * r, r), r), :] for k in range(n_qb)], axis=0
    )
    mid = stack_factor(mid)
    copies[2].wait()
    copies[3].wait()
    for s in range(slabs):
        x, y = slab_of_native(x_ref, s), slab_of_native(y_ref, s)
        z = times_right(jnp.concatenate([x, y], axis=0), low)
        z = times_left(mid, jnp.concatenate([z[:d], z[d:]], axis=1))
        late, i = (0, s) if s < early else (1, s - early)
        for k, out in enumerate(outs[late * n_qb : (late + 1) * n_qb]):
            out[0, i] = z[k * r : (k + 1) * r, :d]
            out[1, i] = z[k * r : (k + 1) * r, d:]


def split_sum_kernel(bit, shared, keep, got, *refs):
    outs, total = refs[:-1], refs[-1]
    total[...] = keep[...] + got[...]
    split_total(bit, shared, outs, total)


def split_total(bit, shared, outs, total):
    axis, weight = bit
    mine = (lax.axis_index(axis) // weight) % 2
    first = total.shape[0] - shared
    for which, out in enumerate(outs):
        half = first // 2
        start = (mine ^ which) * half
        out[:half] = total[pl.ds(pl.multiple_of(start, half), half), :]
        rest = out.shape[0] - half
        if rest and rest == shared:
            out[half:] = total[first:]
        elif rest:
            start = pl.multiple_of(first + (mine ^ which) * rest, rest)
            out[half:] = total[pl.ds(start, rest), :]


def join_split_kernel(bit, keep0, got0, keep1, got1, *refs):
    outs, total = refs[:-1], refs[-1]
    shared = keep1.shape[0]
    total[:-shared] = keep0[...] + got0[...]
    total[-shared:] = keep1[...] + got1[...]
    split_total(bit, shared, outs, total)


def sum_kernel(keep, got, out):
    out[...] = keep[...] + got[...]


def collect_kernel(orders, back, *refs):
    ins, out = refs[:-1], refs[-1]
    size = ins[0].shape[0] // 2
    for i, ref in enumerate(ins):
        for block, order in enumerate(orders):
            row = 0
            for axis, weight in order:
                delta = (i >> back.index((axis, weight))) & 1
                row = row * 2 + ((lax.axis_index(axis) // weight) % 2) ^ delta
            row = pl.multiple_of(row * size, size)
            out[block, pl.ds(row, size), :] = ref[block * size : (block + 1) * size]


def store_kernel(parts, first, second):
    n, _, slabs, r, d = parts.shape
    for a, out in enumerate((first, second)):
        flat = out.reshape(n * r * slabs, d)
        for s in range(slabs):
            flat[pl.ds(s, n * r, stride=slabs), :] = slab_of_parts(parts, a, s)


def place_kernel(n_qa, parts, *refs):
    blocks, outs = refs[:n_qa], refs[n_qa:]
    rows, slabs, d = outs[0].shape
    r, early = rows // n_qa, parts.shape[2]
    for a, out in enumerate(outs):
        flat = out.reshape(rows * slabs, d)
        for s in range(early):
            flat[pl.ds(s, rows, stride=slabs), :] = slab_of_parts(parts, a, s)
    for k, ref in enumerate(blocks):
        start = pl.multiple_of((lax.axis_index("qa") ^ k) * (r * slabs), r * slabs)
        for a, out in enumerate(outs):
            flat = out.reshape(rows * slabs, d)
            for s in range(early, slabs):
                flat[pl.ds(start + s, r, stride=slabs), :] = ref[a, s - early]


def call(kernel, out_shape, inputs, scratch=(), flops=0, far=(), far_out=(), ride=()):
    def spec(i, x):
        near = pltpu.SMEM if x.dtype == jnp.int32 else pltpu.VMEM
        return pl.BlockSpec(memory_space=pl.ANY if i in far else near)

    outs, tree = jax.tree.flatten(out_shape)
    n_in, n_out, n_ride = len(inputs), len(outs), len(ride)
    passing = [pl.BlockSpec(memory_space=pl.ANY)] * n_ride

    def body(*refs):
        rest = refs[n_in + n_ride :]
        kernel(*refs[:n_in], *rest[:n_out], *rest[n_out + n_ride :])

    size = sum(x.size * 4 for x in inputs) + sum(x.size * 4 for x in outs)
    got = pl.pallas_call(
        body,
        out_shape=outs + [shape(*x.shape) for x in ride],
        in_specs=[spec(i, x) for i, x in enumerate(inputs)] + passing,
        out_specs=[pl.BlockSpec(memory_space=pltpu.HBM if i in far_out else pltpu.VMEM) for i in range(n_out)] + passing,
        scratch_shapes=list(scratch),
        input_output_aliases={n_in + i: n_out + i for i in range(n_ride)},
        compiler_params=pltpu.CompilerParams(vmem_limit_bytes=VMEM_LIMIT),
        cost_estimate=pl.CostEstimate(flops=flops, bytes_accessed=size, transcendentals=0),
    )(*inputs, *ride)
    result = jax.tree.unflatten(tree, got[:n_out])
    return (result, list(got[n_out:])) if n_ride else result


def shape(*dims):
    return jax.ShapeDtypeStruct(dims, F32)


def exchange(x, da, db):
    n_qa, n_qb = lax.axis_size("qa"), lax.axis_size("qb")
    pairs = [(a * n_qb + b, (a ^ da) * n_qb + (b ^ db)) for a in range(n_qa) for b in range(n_qb)]
    return lax.ppermute(x, ("qa", "qb"), pairs)


def summed(grads0, grads1):
    both = jnp.stack([grads0, grads1])
    shares = both.reshape(lax.axis_size("qa") * lax.axis_size("qb"), -1, both.shape[-1])
    share = lax.all_to_all(shares, ("qa", "qb"), 0, 0, tiled=True).sum(0, keepdims=True)
    return lax.all_to_all(jnp.broadcast_to(share, shares.shape), ("qa", "qb"), 0, 0, tiled=True)


def nothing(*refs):
    pass


def windows(n_qa):
    ks = sorted(range(1, n_qa), reverse=True)
    stages = WINDOWS
    return {k: stages[min(i, len(stages) - 1)] for i, k in enumerate(ks)}


def shards(state, costate, gates, targets):
    layout = state.shape
    rows, slabs, d = layout[2:]
    n_qa, n_qb = lax.axis_size("qa"), lax.axis_size("qb")
    scale = (n_qa * n_qb * rows * slabs) ** -0.5
    native = shape(*layout[2:])
    natives = [state.reshape(native.shape), costate.reshape(native.shape)]
    r = rows // n_qb
    parts_qa = shape(n_qa, 2, slabs, rows // n_qa, d)
    count = gates.shape[1]
    held, inner = pltpu.VMEM((2, slabs, rows, 2 * d), BF16), pltpu.VMEM((count, d, d), F32)
    def factors(blocks):
        return [(blocks, count, 2 * d, 2 * d), (blocks, count + 1, 2 * d, 2 * d)]

    products0 = shape(count, d, d)
    chain = [pltpu.VMEM(x, BF16) for x in factors(2)] + [pltpu.VMEM((4, d, d), F32)]
    early = slabs // 2
    work = 2 * 2 * 2 * 4 * rows * slabs * d * d
    every = count * d

    if every % (16 * n_qb) or r % 16 or n_qa % 2 or n_qb % 2:
        parts_qb = shape(n_qb, 2, slabs, r, d)
        sent = call(functools.partial(apply_kernel, 1, True), parts_qb, [targets, gates, *natives], flops=work)
        parts = lax.all_to_all(sent, "qb", 0, 0, tiled=True)
        grads1, products = call(
            functools.partial(gradient_kernel, 1, scale),
            [shape(count, d, d), products0], [targets, gates, *natives], [held, inner, *chain], 8 * work,
        )
        sent = call(functools.partial(apply_kernel, 0, False), parts_qa, [targets, gates, parts], flops=work)
        last = lax.all_to_all(sent, "qa", 0, 0, tiled=True)
        first, second = call(store_kernel, (native, native), [last])
        grads0 = call(
            functools.partial(slabs_gradient_kernel, 0, scale),
            shape(count, d, d), [targets, products, parts], [held, inner, *(pltpu.VMEM(x, BF16) for x in factors(1))], 8 * work,
        )
        whole = summed(grads0, grads1)
    else:
        blocks = call(
            functools.partial(first_kernel, 1, n_qb),
            [shape(2, n, r, d) for n in (early, slabs - early) for _ in range(n_qb)],
            [pltpu.with_memory_space_constraint(x, pltpu.HBM) for x in (targets, gates, *natives)],
            [
                pltpu.SMEM(targets.shape, jnp.int32),
                pltpu.VMEM((1, *gates.shape[1:]), F32),
                pltpu.VMEM(native.shape, F32),
                pltpu.VMEM(native.shape, F32),
                pltpu.VMEM((d, d), F32),
                pltpu.SemaphoreType.DMA((4,)),
            ],
            work,
            far=(0, 1, 2, 3),
        )
        front, rear = blocks[:n_qb], blocks[n_qb:]
        front = front[:1] + [exchange(x, 0, k) for k, x in enumerate(front) if k]
        rear = rear[:1] + [exchange(x, 0, k) for k, x in enumerate(rear) if k]
        bits = [("qb", 1 << i) for i in range(n_qb.bit_length() - 1)]
        across_x = ("qa", 1)

        def across(x, bit):
            return exchange(x, bit[1], 0) if bit[0] == "qa" else exchange(x, 0, bit[1])

        half = shape(every // 2, d)
        square = jax.ShapeDtypeStruct((2 * d, 2 * d), BF16)
        keep1, send1, products, low, mid = call(
            functools.partial(first_gradient_kernel, 1, scale),
            [half, half, products0, square, square],
            [targets, gates, *natives],
            [held, inner, *chain, inner, inner, pltpu.SemaphoreType.DMA],
            10 * work,
            far_out=(2,),
        )
        got1 = across(send1, bits[0])
        sent = call(
            functools.partial(early_kernel, n_qb),
            shape(n_qa, 2, early, rows // n_qa, d),
            [low, mid, *front],
            [pltpu.VMEM((2, early, rows, d), F32)],
            3 * work,
        )
        parts = lax.all_to_all(sent, "qa", 0, 0, tiled=True)
        *moved, keep0, send0 = call(
            functools.partial(second_kernel, 0, n_qa, n_qb, early, scale),
            [shape(2, slabs - early, rows // n_qa, d)] * n_qa + [half, half],
            [targets, products, *front, *rear],
            [held, inner, inner, inner, *(pltpu.VMEM(x, BF16) for x in factors(1)), pltpu.SemaphoreType.DMA],
            K0COST * work,
            far=(1,),
        )
        came = {0: moved[0], "parts": parts}
        moved = dict(enumerate(moved))
        window = windows(n_qa)

        def after(stage, kernel, out_shape, inputs, scratch=(), far=()):
            due = [k for k in window if window[k][1] == stage]
            opens = [k for k in window if window[k][0] == stage]
            ride = [came[k] for k in due] + [moved[k] for k in opens]
            if stage == PARTS_DUE:
                ride, due = [came["parts"], *ride], ["parts", *due]
            if not ride:
                return call(kernel, out_shape, inputs, scratch, far=far) if out_shape else None
            result, rode = call(kernel, out_shape, inputs, scratch, far=far, ride=ride)
            came.update(zip(due, rode))
            moved.update(zip(opens, rode[len(due) :]))
            start(stage)
            return result

        def start(stage):
            for k in window:
                if window[k][0] == stage:
                    came[k] = exchange(moved[k], k, 0)

        start(0)
        keep, got = (keep0, keep1), (across(send0, bits[0]), got1)
        bits = bits + [across_x]
        size = every // 2
        for i, bit in enumerate(bits[1:]):
            if i == 0:
                kernel, inputs = functools.partial(join_split_kernel, bit), [keep[0], got[0], keep[1], got[1]]
            else:
                kernel, inputs = functools.partial(split_sum_kernel, bit, size), [keep, got]
            scratch = [pltpu.VMEM((2 * size, d), F32)]
            keep, send = after(i + 1, kernel, [shape(size, d)] * 2, inputs, scratch)
            got = across(send, bit)
            size = size // 2
        mine = after("plane", sum_kernel, shape(*keep.shape), [keep, got])
        for i in range(1, n_qa.bit_length() - 1):
            got = exchange(mine, 1 << i, 0)
            mine = after(("line", i), sum_kernel, shape(*mine.shape), [mine, got])
        back = list(reversed(bits))
        found = [mine]
        for i, bit in enumerate(back):
            found = found + [across(x, bit) for x in found]
            after(("back", i), nothing, [], [found[-1]], far=(0,))
        whole = call(
            functools.partial(collect_kernel, [bits, bits], back), shape(gates.shape[0], every, d), found
        )
        first, second = call(
            functools.partial(place_kernel, n_qa),
            (native, native),
            [came["parts"], *(came[k] for k in range(n_qa))],
        )
    return first.reshape(layout), second.reshape(layout), whole.reshape(gates.shape)


def solution(mesh):
    in_specs = (P("qa", "qb", None, None, None), P("qa", "qb", None, None, None), P(), P())
    out_specs = (P("qa", "qb", None, None, None), P("qa", "qb", None, None, None), P())
    return jax.shard_map(shards, mesh=mesh, in_specs=in_specs, out_specs=out_specs, check_vma=False)
```

```python
import functools

import jax
import jax.numpy as jnp
from jax import lax
from jax.experimental import pallas as pl
from jax.experimental.pallas import tpu as pltpu
from jax.sharding import PartitionSpec as P

F32, BF16 = jnp.float32, jnp.bfloat16
K0COST = 50
WINDOWS = [(0, ('line', 1)), (1, ('line', 1)), ('plane', ('line', 2)), (('line', 1), None), (('line', 1), None), ('plane', ('line', 2)), ('plane', ('back', 0))]
VMEM_LIMIT = 16 * 1024 * 1024


def split(x):
    high = x.astype(BF16)
    return high, (x - high.astype(F32)).astype(BF16)


def dot(a, b, dims=((1,), (0,))):
    return lax.dot_general(a, b, (dims, ((), ())), preferred_element_type=F32)


def right_factor(u):
    high, low = split(u)
    row = jnp.concatenate([high, low], axis=1)
    return jnp.concatenate([row, row], axis=0)


def left_factor(u):
    return stack_factor(jnp.transpose(u))


def stack_factor(u):
    high, low = split(u)
    return jnp.concatenate(
        [jnp.concatenate([high, high], axis=1), jnp.concatenate([low, low], axis=1)], axis=0
    )


def times_right(x, factor):
    d = x.shape[1]
    r = dot(jnp.concatenate(split(x), axis=1), factor)
    return r[:, :d] + r[:, d:]


def times_left(factor, x):
    d = x.shape[0]
    r = dot(factor, jnp.concatenate(split(x), axis=0))
    return r[:d] + r[d:]


def matmul(a, b):
    return times_right(a, right_factor(b))


def slab_of_native(ref, s):
    rows, slabs, lanes = ref.shape
    return ref.reshape(rows * slabs, lanes)[pl.ds(s, rows, stride=slabs), :]


def slab_of_parts(ref, a, s):
    n, _, _, r, lanes = ref.shape
    return ref[:, a, s].reshape(n * r, lanes)


def products(targets, gates, block, at):
    d = gates.shape[-1]
    eye = (
        lax.broadcasted_iota(jnp.int32, (d, d), 0) == lax.broadcasted_iota(jnp.int32, (d, d), 1)
    ).astype(F32)
    last = gates.shape[1] - 1
    u = gates[at, last]
    low_turn = targets[block, last] == 0
    low, mid = jnp.where(low_turn, u, eye), jnp.where(low_turn, eye, u)
    for g in range(last - 1, -1, -1):
        both = matmul(jnp.concatenate([low, mid], axis=0), gates[at, g])
        low_turn = targets[block, g] == 0
        low, mid = jnp.where(low_turn, both[:d], low), jnp.where(low_turn, mid, both[d:])
    return low, mid


def apply_kernel(block, native, targets, gates, *refs):
    out = refs[-1]
    n, _, slabs, r, d = out.shape
    low, mid = products(targets, gates, block, block)
    low, mid = right_factor(low), left_factor(mid)
    for s in range(slabs):
        if native:
            x, y = slab_of_native(refs[0], s), slab_of_native(refs[1], s)
        else:
            x, y = slab_of_parts(refs[0], 0, s), slab_of_parts(refs[0], 1, s)
        z = times_right(jnp.concatenate([x, y], axis=0), low)
        z = times_left(mid, jnp.concatenate([z[: n * r], z[n * r :]], axis=1))
        out[:, 0, s] = z[:, :d].reshape(n, r, d)
        out[:, 1, s] = z[:, d:].reshape(n, r, d)


def fuse(x):
    return jnp.concatenate(split(x), axis=-1)


def stacked(x):
    d = x.shape[-1] // 2
    return jnp.concatenate([x[:, :d], x[:, d:]], axis=0)


def same_run(targets, block, g):
    return targets[block, g] == targets[block, g + 1]


def identity(d):
    rows, columns = (lax.broadcasted_iota(jnp.int32, (d, d), i) for i in range(2))
    return (rows == columns).astype(F32)


def chains(targets, gates, right, left, made, kept):
    blocks, count, d, _ = gates.shape
    eye = identity(d)
    left[1, count] = left_factor(eye)

    def keep(block, g, p):
        made[block] = p
        if block:
            right[block, g] = right_factor(p)
            left[block, g] = left_factor(p)
        else:
            kept[g] = p

    for block in range(blocks):
        keep(block, count - 1, gates[block, count - 1])
    low_turn = targets[0, count - 1] == 0
    made[blocks] = jnp.where(low_turn, gates[0, count - 1], eye)
    made[blocks + 1] = jnp.where(low_turn, eye, gates[0, count - 1])

    def step(i, _):
        g = count - 1 - i
        for block in range(blocks):
            u = gates[block, g]
            going = targets[block, g] == targets[block, g + 1]
            keep(block, g, jnp.where(going, matmul(made[block], u), u))
        both = made[pl.ds(blocks, 2)].reshape(2 * d, d)
        both = matmul(both, gates[0, g])
        low_turn = targets[0, g] == 0
        made[blocks] = jnp.where(low_turn, both[:d], made[blocks])
        made[blocks + 1] = jnp.where(low_turn, made[blocks + 1], both[d:])
        return _

    lax.fori_loop(1, count, step, 0)


def block_kernel(block, at, scale, targets, right, left, held, inner, grads):
    _, slabs, rows, d = held.shape
    d = d // 2
    count = grads.shape[0]

    def contract_low():
        y, x = (held[a].reshape(slabs * rows, 2 * d) for a in (1, 0))
        return dot(y, x, ((0,), (0,)))

    def contract_mid():
        y, x = (
            jnp.concatenate([stacked(held[a, s]) for s in range(slabs)], axis=1) for a in (1, 0)
        )
        return dot(y, x, ((1,), (1,)))

    def contract(g, how):
        total = how()
        inner[g] = (total[:d, :d] + total[d:, d:]) + (total[:d, d:] + total[d:, :d])

    def apply_low(g, begin=0):
        step = slabs // 2
        for a in range(2):
            for s in range(begin, slabs, step):
                r = dot(held[a, pl.ds(s, step)].reshape(step * rows, 2 * d), right[at, g])
                held[a, pl.ds(s, step)] = fuse((r[:, :d] + r[:, d:]).reshape(step, rows, d))

    def apply_mid(g):
        for s in range(0, slabs, 2):
            pairs = [(a, s + j) for a in range(2) for j in range(2)]
            x = jnp.concatenate([stacked(held[pair]) for pair in pairs], axis=1)
            r = dot(left[at, g], x)
            r = r[:d] + r[d:]
            for j, pair in enumerate(pairs):
                held[pair] = fuse(r[:, j * d : (j + 1) * d])

    def step(i, _):
        g = count - 1 - i
        low_turn = targets[block, g] == 0
        mid_turn = jnp.logical_not(low_turn)
        fresh = jnp.logical_or(i == 0, targets[block, g] != targets[block, jnp.minimum(g + 1, count - 1)])
        pl.when(jnp.logical_and(fresh, low_turn))(lambda: contract(g, contract_low))
        pl.when(jnp.logical_and(fresh, mid_turn))(lambda: contract(g, contract_mid))
        turn = targets[block, g] != targets[block, jnp.maximum(g - 1, 0)]
        pl.when(jnp.logical_and(turn, low_turn))(lambda: apply_low(g))
        pl.when(jnp.logical_and(turn, mid_turn))(lambda: apply_mid(g))
        return _

    lax.fori_loop(0, count, step, 0)
    first = [count - 1] * count
    before = [count] * count
    for g in range(count - 2, -1, -1):
        going = same_run(targets, block, g)
        first[g] = jnp.where(going, first[g + 1], g)
        before[g] = jnp.where(going, g + 1, count)
    moved = [times_right(inner[first[g]], right[at, g]) for g in range(count)]
    for g in range(count):
        grads[g] = times_left(left[at, before[g]], moved[g]) * scale


def halves(grads, keep, send):
    half = grads.shape[0] // 2
    core = lax.axis_index("qb") % 2
    keep[...] = grads[pl.ds(core * half, half)].reshape(keep.shape)
    send[...] = grads[pl.ds((1 - core) * half, half)].reshape(send.shape)


def first_gradient_kernel(block, scale, *refs):
    refs, (keep, send, right0, left0, low0, mid0, held, inner, right, left, made, grads, products) = refs[:4], refs[4:]
    gradient_kernel(block, scale, *refs, grads, products, held, inner, right, left, made)
    build(products, right0, left0)
    low0[...] = right_factor(made[made.shape[0] - 2])
    mid0[...] = left_factor(made[made.shape[0] - 1])
    halves(grads, keep, send)


def build(products, right, left):
    count, d, _ = products.shape
    for g in range(count):
        right[0, g] = right_factor(products[g])
        left[0, g] = left_factor(products[g])
    left[0, count] = left_factor(identity(d))


def gradient_kernel(block, scale, targets, gates, state, costate, out, factors0, held, inner, right, left, made):
    chains(targets, gates, right, left, made, factors0)
    for s in range(held.shape[1]):
        for a, ref in enumerate((state, costate)):
            held[a, s] = fuse(slab_of_native(ref, s))
    block_kernel(block, block, scale, targets, right, left, held, inner, out)


def slabs_gradient_kernel(block, scale, targets, products, parts, out, held, inner, right, left):
    build(products, right, left)
    for s in range(held.shape[1]):
        for a in range(2):
            held[a, s] = fuse(slab_of_parts(parts, a, s))
    block_kernel(block, 0, scale, targets, right, left, held, inner, out)


def end_kernel(n_qb, low, mid, *refs):
    blocks, outs, held = refs[:n_qb], refs[n_qb:-1], refs[-1]
    gather(blocks, lambda rows, x: held.__setitem__((slice(None), slice(None), rows), x))
    _, slabs, rows, d = held.shape
    for s in range(slabs):
        z = times_right(jnp.concatenate([held[0, s], held[1, s]], axis=0), low[...])
        z = times_left(mid[...], jnp.concatenate([z[:rows], z[rows:]], axis=1))
        held[0, s] = z[:, :d]
        held[1, s] = z[:, d:]
    for k, ref in enumerate(outs):
        count = ref.shape[2]
        start = (lax.axis_index("qa") ^ k) * count
        ref[...] = held[:, :, pl.ds(pl.multiple_of(start, count), count)]


def gather(blocks, put):
    mine = lax.axis_index("qb")
    for k, ref in enumerate(blocks):
        count = ref.shape[2]
        put(pl.ds(pl.multiple_of((mine ^ k) * count, count), count), ref[...])


def second_kernel(block, n_qb, scale, targets, right, left, *refs):
    blocks = refs[:n_qb]
    keep, send, held, inner, grads = refs[n_qb:]
    gather(blocks, lambda rows, x: held.__setitem__((slice(None), slice(None), rows), fuse(x)))
    block_kernel(block, 0, scale, targets, right, left, held, inner, grads)
    halves(grads, keep, send)


def first_kernel(block, n_qb, far_targets, gates, state, costate, *refs):
    outs, (targets, mats, x_ref, y_ref, turned, sems) = refs[:n_qb], refs[n_qb:]
    copies = [
        pltpu.make_async_copy(far_targets, targets, sems.at[3]),
        pltpu.make_async_copy(gates.at[pl.ds(block, 1)], mats, sems.at[0]),
        pltpu.make_async_copy(state, x_ref, sems.at[1]),
        pltpu.make_async_copy(costate, y_ref, sems.at[2]),
    ]
    for copy in copies:
        copy.start()
    _, slabs, r, d = outs[0].shape
    mine = lax.axis_index("qb")
    copies[0].wait()
    copies[1].wait()
    low, mid = products(targets, mats, block, 0)
    low = right_factor(low)
    turned[...] = jnp.transpose(mid)
    mid = jnp.concatenate(
        [turned[pl.ds(pl.multiple_of((mine ^ k) * r, r), r), :] for k in range(n_qb)], axis=0
    )
    mid = stack_factor(mid)
    copies[2].wait()
    copies[3].wait()
    for s in range(slabs):
        x, y = slab_of_native(x_ref, s), slab_of_native(y_ref, s)
        z = times_right(jnp.concatenate([x, y], axis=0), low)
        z = times_left(mid, jnp.concatenate([z[:d], z[d:]], axis=1))
        for k, out in enumerate(outs):
            out[0, s] = z[k * r : (k + 1) * r, :d]
            out[1, s] = z[k * r : (k + 1) * r, d:]


def plane_partners(n_qb):
    return [(dx, dy) for dx in range(2) for dy in range(n_qb // 2)]


def place_of(n_qb, dx, dy):
    x, y = lax.axis_index("qa") % 2, lax.axis_index("qb") // 2
    return (x ^ dx) * (n_qb // 2) + (y ^ dy)


def spread_kernel(n_qb, *refs):
    pairs, (*outs, total) = refs[:4], refs[4:]
    for block in range(2):
        total[block] = pairs[2 * block][...] + pairs[2 * block + 1][...]
    size = total.shape[1] // n_qb
    for (dx, dy), out in zip(plane_partners(n_qb), outs):
        rows = pl.ds(pl.multiple_of(place_of(n_qb, dx, dy) * size, size), size)
        for block in range(2):
            out[block * size : (block + 1) * size] = total[block, rows]


def plane_sum_kernel(*refs):
    refs[-1][...] = functools.reduce(lambda a, b: a + b, [ref[...] for ref in refs[:-1]])


def sum_kernel(keep, got, out):
    out[...] = keep[...] + got[...]


def collect_kernel(n_qb, *refs):
    ins, (out, held, sem) = refs[:-3], refs[-3:]
    size = ins[0].shape[0] // 2
    copies = []
    for block in range(2):
        for i, ref in enumerate(ins):
            core = (lax.axis_index("qb") % 2) ^ (i // n_qb)
            row = core * n_qb + place_of(n_qb, *plane_partners(n_qb)[i % n_qb])
            rows = pl.ds(pl.multiple_of(row * size, size), size)
            held[block, rows] = ref[block * size : (block + 1) * size]
        copies.append(pltpu.make_async_copy(held.at[block], out.at[block], sem.at[block]))
        copies[-1].start()
    for copy in copies:
        copy.wait()


def store_kernel(parts, first, second):
    n, _, slabs, r, d = parts.shape
    for a, out in enumerate((first, second)):
        flat = out.reshape(n * r * slabs, d)
        for s in range(slabs):
            flat[pl.ds(s, n * r, stride=slabs), :] = slab_of_parts(parts, a, s)


def place_kernel(n_qa, *refs):
    blocks, (*outs, held, sem) = refs[:n_qa], refs[n_qa:]
    _, rows, slabs, d = held.shape
    r = rows // n_qa
    copies = []
    for a, out in enumerate(outs):
        flat = held.at[a].reshape(rows * slabs, d)
        for k, ref in enumerate(blocks):
            start = pl.multiple_of((lax.axis_index("qa") ^ k) * (r * slabs), r * slabs)
            for s in range(slabs):
                flat[pl.ds(start + s, r, stride=slabs), :] = ref[a, s]
        copies.append(pltpu.make_async_copy(held.at[a], out, sem.at[a]))
        copies[-1].start()
    for copy in copies:
        copy.wait()


def call(kernel, out_shape, inputs, scratch=(), flops=0, far=(), far_out=(), ride=()):
    def spec(i, x):
        near = pltpu.SMEM if x.dtype == jnp.int32 else pltpu.VMEM
        return pl.BlockSpec(memory_space=pl.ANY if i in far else near)

    outs, tree = jax.tree.flatten(out_shape)
    n_in, n_out, n_ride = len(inputs), len(outs), len(ride)
    passing = [pl.BlockSpec(memory_space=pl.ANY)] * n_ride

    def body(*refs):
        rest = refs[n_in + n_ride :]
        kernel(*refs[:n_in], *rest[:n_out], *rest[n_out + n_ride :])

    size = sum(x.size * 4 for x in inputs) + sum(x.size * 4 for x in outs)
    got = pl.pallas_call(
        body,
        out_shape=outs + [shape(*x.shape) for x in ride],
        in_specs=[spec(i, x) for i, x in enumerate(inputs)] + passing,
        out_specs=[pl.BlockSpec(memory_space=pltpu.HBM if i in far_out else pltpu.VMEM) for i in range(n_out)] + passing,
        scratch_shapes=list(scratch),
        input_output_aliases={n_in + i: n_out + i for i in range(n_ride)},
        compiler_params=pltpu.CompilerParams(vmem_limit_bytes=VMEM_LIMIT),
        cost_estimate=pl.CostEstimate(flops=flops, bytes_accessed=size, transcendentals=0),
    )(*inputs, *ride)
    result = jax.tree.unflatten(tree, got[:n_out])
    return (result, list(got[n_out:])) if n_ride else result


def shape(*dims):
    return jax.ShapeDtypeStruct(dims, F32)


def exchange(x, da, db):
    n_qa, n_qb = lax.axis_size("qa"), lax.axis_size("qb")
    pairs = [(a * n_qb + b, (a ^ da) * n_qb + (b ^ db)) for a in range(n_qa) for b in range(n_qb)]
    return lax.ppermute(x, ("qa", "qb"), pairs)


def summed(grads0, grads1):
    both = jnp.stack([grads0, grads1])
    shares = both.reshape(lax.axis_size("qa") * lax.axis_size("qb"), -1, both.shape[-1])
    share = lax.all_to_all(shares, ("qa", "qb"), 0, 0, tiled=True).sum(0, keepdims=True)
    return lax.all_to_all(jnp.broadcast_to(share, shares.shape), ("qa", "qb"), 0, 0, tiled=True)


def nothing(*refs):
    pass


def windows(n_qa):
    ks = sorted(range(1, n_qa), reverse=True)
    stages = WINDOWS
    return {k: stages[min(i, len(stages) - 1)] for i, k in enumerate(ks)}


def shards(state, costate, gates, targets):
    layout = state.shape
    rows, slabs, d = layout[2:]
    n_qa, n_qb = lax.axis_size("qa"), lax.axis_size("qb")
    scale = (n_qa * n_qb * rows * slabs) ** -0.5
    native = shape(*layout[2:])
    natives = [state.reshape(native.shape), costate.reshape(native.shape)]
    r = rows // n_qb
    parts_qa = shape(n_qa, 2, slabs, rows // n_qa, d)
    count = gates.shape[1]
    held, inner = pltpu.VMEM((2, slabs, rows, 2 * d), BF16), pltpu.VMEM((count, d, d), F32)
    def factors(blocks):
        return [(blocks, count, 2 * d, 2 * d), (blocks, count + 1, 2 * d, 2 * d)]

    products0 = shape(count, d, d)
    chain = [pltpu.VMEM(x, BF16) for x in factors(2)] + [pltpu.VMEM((4, d, d), F32)]
    work = 2 * 2 * 2 * 4 * rows * slabs * d * d
    every = count * d

    if every % (16 * n_qb) or r % 16 or n_qa % 2 or n_qb % 2:
        parts_qb = shape(n_qb, 2, slabs, r, d)
        sent = call(functools.partial(apply_kernel, 1, True), parts_qb, [targets, gates, *natives], flops=work)
        parts = lax.all_to_all(sent, "qb", 0, 0, tiled=True)
        grads1, products = call(
            functools.partial(gradient_kernel, 1, scale),
            [shape(count, d, d), products0], [targets, gates, *natives], [held, inner, *chain], 8 * work,
        )
        sent = call(functools.partial(apply_kernel, 0, False), parts_qa, [targets, gates, parts], flops=work)
        last = lax.all_to_all(sent, "qa", 0, 0, tiled=True)
        first, second = call(store_kernel, (native, native), [last])
        grads0 = call(
            functools.partial(slabs_gradient_kernel, 0, scale),
            shape(count, d, d), [targets, products, parts], [held, inner, *(pltpu.VMEM(x, BF16) for x in factors(1))], 8 * work,
        )
        whole = summed(grads0, grads1)
    else:
        blocks = call(
            functools.partial(first_kernel, 1, n_qb),
            [shape(2, slabs, r, d)] * n_qb,
            [pltpu.with_memory_space_constraint(x, pltpu.HBM) for x in (targets, gates, *natives)],
            [
                pltpu.SMEM(targets.shape, jnp.int32),
                pltpu.VMEM((1, *gates.shape[1:]), F32),
                pltpu.VMEM(native.shape, F32),
                pltpu.VMEM(native.shape, F32),
                pltpu.VMEM((d, d), F32),
                pltpu.SemaphoreType.DMA((4,)),
            ],
            work,
            far=(0, 1, 2, 3),
        )
        blocks = blocks[:1] + [exchange(x, 0, k) for k, x in enumerate(blocks) if k]
        half = shape(every // 2, d)
        square = jax.ShapeDtypeStruct((2 * d, 2 * d), BF16)
        keep1, send1, right0, left0, low, mid = call(
            functools.partial(first_gradient_kernel, 1, scale),
            [half, half, *(jax.ShapeDtypeStruct(x, BF16) for x in factors(1)), square, square],
            [targets, gates, *natives],
            [held, inner, *chain, inner, inner],
            10 * work,
        )
        got1 = exchange(send1, 0, 1)
        keep0, send0 = call(
            functools.partial(second_kernel, 0, n_qb, scale),
            [half, half],
            [targets, right0, left0, *blocks],
            [held, inner, inner],
            K0COST * work,
        )
        got0 = exchange(send0, 0, 1)
        moved, _ = call(
            functools.partial(end_kernel, n_qb),
            [shape(2, slabs, rows // n_qa, d)] * n_qa,
            [low, mid, *blocks],
            [pltpu.VMEM((2, slabs, rows, d), F32)],
            3 * work,
            ride=[keep0],
        )
        came = {0: moved[0]}
        moved = dict(enumerate(moved))
        window = windows(n_qa)

        def after(stage, kernel, out_shape, inputs, scratch=(), far=()):
            due = [k for k in window if window[k][1] == stage]
            opens = [k for k in window if window[k][0] == stage]
            ride = [came[k] for k in due] + [moved[k] for k in opens]
            if not ride:
                return call(kernel, out_shape, inputs, scratch, far=far) if out_shape else None
            result, rode = call(kernel, out_shape, inputs, scratch, far=far, ride=ride)
            came.update(zip(due, rode))
            moved.update(zip(opens, rode[len(due) :]))
            start(stage)
            return result

        def start(stage):
            for k in window:
                if window[k][0] == stage:
                    came[k] = exchange(moved[k], k, 0)

        start(0)
        partners = plane_partners(n_qb)
        size = every // n_qb
        pieces = after(
            1,
            functools.partial(spread_kernel, n_qb),
            [shape(size, d)] * n_qb,
            [keep0, got0, keep1, got1],
            [pltpu.VMEM((2, every // 2, d), F32)],
        )
        pieces = pieces[:1] + [exchange(x, dx, 2 * dy) for x, (dx, dy) in zip(pieces[1:], partners[1:])]
        mine = after("plane", plane_sum_kernel, shape(size, d), pieces)
        for i in range(1, n_qa.bit_length() - 1):
            got = exchange(mine, 1 << i, 0)
            mine = after(("line", i), sum_kernel, shape(*mine.shape), [mine, got])
        found = [mine] + [exchange(mine, dx, 2 * dy) for dx, dy in partners[1:]]
        after(("back", 0), nothing, [], [found[1]], far=(0,))
        after(("back", 1), nothing, [], [found[-1]], far=(0,))
        found = found + [exchange(x, 0, 1) for x in found]
        whole = call(
            functools.partial(collect_kernel, n_qb),
            shape(gates.shape[0], every, d),
            found,
            [pltpu.VMEM((gates.shape[0], every, d), F32), pltpu.SemaphoreType.DMA((2,))],
            far_out=(0,),
        )
        first, second = call(
            functools.partial(place_kernel, n_qa),
            (native, native),
            [came[k] for k in range(n_qa)],
            [pltpu.VMEM((2, *native.shape), F32), pltpu.SemaphoreType.DMA((2,))],
            far_out=(0, 1),
        )
    return first.reshape(layout), second.reshape(layout), whole.reshape(gates.shape)


def solution(mesh):
    in_specs = (P("qa", "qb", None, None, None), P("qa", "qb", None, None, None), P(), P())
    out_specs = (P("qa", "qb", None, None, None), P("qa", "qb", None, None, None), P())
    return jax.shard_map(shards, mesh=mesh, in_specs=in_specs, out_specs=out_specs, check_vma=False)
```

```python
import functools

import jax
import jax.numpy as jnp
from jax import lax
from jax.experimental import pallas as pl
from jax.experimental.pallas import tpu as pltpu
from jax.sharding import PartitionSpec as P

F32, BF16 = jnp.float32, jnp.bfloat16
K0COST = 50
WINDOWS = [(0, ('line', 1)), (1, ('line', 1)), ('plane', ('line', 2)), (('line', 1), None), (('line', 1), None), ('plane', ('line', 2)), ('plane', ('back', 0))]
VMEM_LIMIT = 16 * 1024 * 1024


def split(x):
    high = x.astype(BF16)
    return high, (x - high.astype(F32)).astype(BF16)


def dot(a, b, dims=((1,), (0,))):
    return lax.dot_general(a, b, (dims, ((), ())), preferred_element_type=F32)


def right_factor(u):
    high, low = split(u)
    row = jnp.concatenate([high, low], axis=1)
    return jnp.concatenate([row, row], axis=0)


def left_factor(u):
    return stack_factor(jnp.transpose(u))


def stack_factor(u):
    high, low = split(u)
    return jnp.concatenate(
        [jnp.concatenate([high, high], axis=1), jnp.concatenate([low, low], axis=1)], axis=0
    )


def times_right(x, factor):
    d = x.shape[1]
    r = dot(jnp.concatenate(split(x), axis=1), factor)
    return r[:, :d] + r[:, d:]


def times_left(factor, x):
    d = x.shape[0]
    r = dot(factor, jnp.concatenate(split(x), axis=0))
    return r[:d] + r[d:]


def matmul(a, b):
    return times_right(a, right_factor(b))


def slab_of_native(ref, s):
    rows, slabs, lanes = ref.shape
    return ref.reshape(rows * slabs, lanes)[pl.ds(s, rows, stride=slabs), :]


def slab_of_parts(ref, a, s):
    n, _, _, r, lanes = ref.shape
    return ref[:, a, s].reshape(n * r, lanes)


def products(targets, gates, block, at):
    d = gates.shape[-1]
    eye = (
        lax.broadcasted_iota(jnp.int32, (d, d), 0) == lax.broadcasted_iota(jnp.int32, (d, d), 1)
    ).astype(F32)
    last = gates.shape[1] - 1
    u = gates[at, last]
    low_turn = targets[block, last] == 0
    low, mid = jnp.where(low_turn, u, eye), jnp.where(low_turn, eye, u)
    for g in range(last - 1, -1, -1):
        both = matmul(jnp.concatenate([low, mid], axis=0), gates[at, g])
        low_turn = targets[block, g] == 0
        low, mid = jnp.where(low_turn, both[:d], low), jnp.where(low_turn, mid, both[d:])
    return low, mid


def apply_kernel(block, native, targets, gates, *refs):
    out = refs[-1]
    n, _, slabs, r, d = out.shape
    low, mid = products(targets, gates, block, block)
    low, mid = right_factor(low), left_factor(mid)
    for s in range(slabs):
        if native:
            x, y = slab_of_native(refs[0], s), slab_of_native(refs[1], s)
        else:
            x, y = slab_of_parts(refs[0], 0, s), slab_of_parts(refs[0], 1, s)
        z = times_right(jnp.concatenate([x, y], axis=0), low)
        z = times_left(mid, jnp.concatenate([z[: n * r], z[n * r :]], axis=1))
        out[:, 0, s] = z[:, :d].reshape(n, r, d)
        out[:, 1, s] = z[:, d:].reshape(n, r, d)


def fuse(x):
    return jnp.concatenate(split(x), axis=-1)


def stacked(x):
    d = x.shape[-1] // 2
    return jnp.concatenate([x[:, :d], x[:, d:]], axis=0)


def same_run(targets, block, g):
    return targets[block, g] == targets[block, g + 1]


def identity(d):
    rows, columns = (lax.broadcasted_iota(jnp.int32, (d, d), i) for i in range(2))
    return (rows == columns).astype(F32)


def chains(targets, gates, right, left, made, kept):
    blocks, count, d, _ = gates.shape
    eye = identity(d)
    left[1, count] = left_factor(eye)

    def keep(block, g, p):
        made[block] = p
        if block:
            right[block, g] = right_factor(p)
            left[block, g] = left_factor(p)
        else:
            kept[g] = p

    for block in range(blocks):
        keep(block, count - 1, gates[block, count - 1])
    low_turn = targets[0, count - 1] == 0
    made[blocks] = jnp.where(low_turn, gates[0, count - 1], eye)
    made[blocks + 1] = jnp.where(low_turn, eye, gates[0, count - 1])

    def step(i, _):
        g = count - 1 - i
        for block in range(blocks):
            u = gates[block, g]
            going = targets[block, g] == targets[block, g + 1]
            keep(block, g, jnp.where(going, matmul(made[block], u), u))
        both = made[pl.ds(blocks, 2)].reshape(2 * d, d)
        both = matmul(both, gates[0, g])
        low_turn = targets[0, g] == 0
        made[blocks] = jnp.where(low_turn, both[:d], made[blocks])
        made[blocks + 1] = jnp.where(low_turn, made[blocks + 1], both[d:])
        return _

    lax.fori_loop(1, count, step, 0)


def block_kernel(block, at, scale, targets, right, left, held, inner, grads):
    _, slabs, rows, d = held.shape
    d = d // 2
    count = grads.shape[0]

    def contract_low():
        y, x = (held[a].reshape(slabs * rows, 2 * d) for a in (1, 0))
        return dot(y, x, ((0,), (0,)))

    def contract_mid():
        y, x = (
            jnp.concatenate([stacked(held[a, s]) for s in range(slabs)], axis=1) for a in (1, 0)
        )
        return dot(y, x, ((1,), (1,)))

    def contract(g, how):
        total = how()
        inner[g] = (total[:d, :d] + total[d:, d:]) + (total[:d, d:] + total[d:, :d])

    def apply_low(g, begin=0):
        step = slabs // 2
        for a in range(2):
            for s in range(begin, slabs, step):
                r = dot(held[a, pl.ds(s, step)].reshape(step * rows, 2 * d), right[at, g])
                held[a, pl.ds(s, step)] = fuse((r[:, :d] + r[:, d:]).reshape(step, rows, d))

    def apply_mid(g):
        for s in range(0, slabs, 2):
            pairs = [(a, s + j) for a in range(2) for j in range(2)]
            x = jnp.concatenate([stacked(held[pair]) for pair in pairs], axis=1)
            r = dot(left[at, g], x)
            r = r[:d] + r[d:]
            for j, pair in enumerate(pairs):
                held[pair] = fuse(r[:, j * d : (j + 1) * d])

    def step(i, _):
        g = count - 1 - i
        low_turn = targets[block, g] == 0
        mid_turn = jnp.logical_not(low_turn)
        fresh = jnp.logical_or(i == 0, targets[block, g] != targets[block, jnp.minimum(g + 1, count - 1)])
        pl.when(jnp.logical_and(fresh, low_turn))(lambda: contract(g, contract_low))
        pl.when(jnp.logical_and(fresh, mid_turn))(lambda: contract(g, contract_mid))
        turn = targets[block, g] != targets[block, jnp.maximum(g - 1, 0)]
        pl.when(jnp.logical_and(turn, low_turn))(lambda: apply_low(g))
        pl.when(jnp.logical_and(turn, mid_turn))(lambda: apply_mid(g))
        return _

    lax.fori_loop(0, count, step, 0)
    first = [count - 1] * count
    before = [count] * count
    for g in range(count - 2, -1, -1):
        going = same_run(targets, block, g)
        first[g] = jnp.where(going, first[g + 1], g)
        before[g] = jnp.where(going, g + 1, count)
    moved = [times_right(inner[first[g]], right[at, g]) for g in range(count)]
    for g in range(count):
        grads[g] = times_left(left[at, before[g]], moved[g]) * scale


def halves(grads, keep, send):
    half = grads.shape[0] // 2
    core = lax.axis_index("qb") % 2
    keep[...] = grads[pl.ds(core * half, half)].reshape(keep.shape)
    send[...] = grads[pl.ds((1 - core) * half, half)].reshape(send.shape)


def first_gradient_kernel(block, scale, *refs):
    refs, (keep, send, right0, left0, low0, mid0, held, inner, right, left, made, grads, products) = refs[:4], refs[4:]
    gradient_kernel(block, scale, *refs, grads, products, held, inner, right, left, made)
    build(products, right0, left0)
    low0[...] = right_factor(made[made.shape[0] - 2])
    mid0[...] = left_factor(made[made.shape[0] - 1])
    halves(grads, keep, send)


def build(products, right, left):
    count, d, _ = products.shape
    for g in range(count):
        right[0, g] = right_factor(products[g])
        left[0, g] = left_factor(products[g])
    left[0, count] = left_factor(identity(d))


def gradient_kernel(block, scale, targets, gates, state, costate, out, factors0, held, inner, right, left, made):
    chains(targets, gates, right, left, made, factors0)
    for s in range(held.shape[1]):
        for a, ref in enumerate((state, costate)):
            held[a, s] = fuse(slab_of_native(ref, s))
    block_kernel(block, block, scale, targets, right, left, held, inner, out)


def slabs_gradient_kernel(block, scale, targets, products, parts, out, held, inner, right, left):
    build(products, right, left)
    for s in range(held.shape[1]):
        for a in range(2):
            held[a, s] = fuse(slab_of_parts(parts, a, s))
    block_kernel(block, 0, scale, targets, right, left, held, inner, out)


def end_kernel(n_qb, low, mid, *refs):
    blocks, outs, held = refs[:n_qb], refs[n_qb:-1], refs[-1]
    gather(blocks, lambda rows, x: held.__setitem__((slice(None), slice(None), rows), x))
    _, slabs, rows, d = held.shape
    for s in range(slabs):
        z = times_right(jnp.concatenate([held[0, s], held[1, s]], axis=0), low[...])
        z = times_left(mid[...], jnp.concatenate([z[:rows], z[rows:]], axis=1))
        held[0, s] = z[:, :d]
        held[1, s] = z[:, d:]
    for k, ref in enumerate(outs):
        count = ref.shape[2]
        start = (lax.axis_index("qa") ^ k) * count
        ref[...] = held[:, :, pl.ds(pl.multiple_of(start, count), count)]


def gather(blocks, put):
    mine = lax.axis_index("qb")
    for k, ref in enumerate(blocks):
        count = ref.shape[2]
        put(pl.ds(pl.multiple_of((mine ^ k) * count, count), count), ref[...])


def second_kernel(block, n_qb, scale, targets, right, left, *refs):
    blocks = refs[:n_qb]
    keep, send, held, inner, grads = refs[n_qb:]
    gather(blocks, lambda rows, x: held.__setitem__((slice(None), slice(None), rows), fuse(x)))
    block_kernel(block, 0, scale, targets, right, left, held, inner, grads)
    halves(grads, keep, send)


def first_kernel(block, n_qb, far_targets, gates, state, costate, *refs):
    outs, (targets, mats, x_ref, y_ref, turned, sems) = refs[:n_qb], refs[n_qb:]
    copies = [
        pltpu.make_async_copy(far_targets, targets, sems.at[3]),
        pltpu.make_async_copy(gates.at[pl.ds(block, 1)], mats, sems.at[0]),
        pltpu.make_async_copy(state, x_ref, sems.at[1]),
        pltpu.make_async_copy(costate, y_ref, sems.at[2]),
    ]
    for copy in copies:
        copy.start()
    _, slabs, r, d = outs[0].shape
    mine = lax.axis_index("qb")
    copies[0].wait()
    copies[1].wait()
    low, mid = products(targets, mats, block, 0)
    low = right_factor(low)
    turned[...] = jnp.transpose(mid)
    mid = jnp.concatenate(
        [turned[pl.ds(pl.multiple_of((mine ^ k) * r, r), r), :] for k in range(n_qb)], axis=0
    )
    mid = stack_factor(mid)
    copies[2].wait()
    copies[3].wait()
    for s in range(slabs):
        x, y = slab_of_native(x_ref, s), slab_of_native(y_ref, s)
        z = times_right(jnp.concatenate([x, y], axis=0), low)
        z = times_left(mid, jnp.concatenate([z[:d], z[d:]], axis=1))
        for k, out in enumerate(outs):
            out[0, s] = z[k * r : (k + 1) * r, :d]
            out[1, s] = z[k * r : (k + 1) * r, d:]


def plane_partners(n_qb):
    pairs = [(dx, dy) for dx in range(2) for dy in range(n_qb // 2)]
    return sorted(pairs, key=lambda p: (p[0] > 0, p[0] * -p[1] if p[0] else p[1]))


def place_of(n_qb, dx, dy):
    x, y = lax.axis_index("qa") % 2, lax.axis_index("qb") // 2
    return (x ^ dx) * (n_qb // 2) + (y ^ dy)


def spread_kernel(n_qb, *refs):
    pairs, (*outs, total) = refs[:4], refs[4:]
    for block in range(2):
        total[block] = pairs[2 * block][...] + pairs[2 * block + 1][...]
    size = total.shape[1] // n_qb
    for (dx, dy), out in zip(plane_partners(n_qb), outs):
        rows = pl.ds(pl.multiple_of(place_of(n_qb, dx, dy) * size, size), size)
        for block in range(2):
            out[block * size : (block + 1) * size] = total[block, rows]


def plane_sum_kernel(*refs):
    refs[-1][...] = functools.reduce(lambda a, b: a + b, [ref[...] for ref in refs[:-1]])


def sum_kernel(keep, got, out):
    out[...] = keep[...] + got[...]


def collect_kernel(n_qb, *refs):
    ins, (out, held, sem) = refs[:-3], refs[-3:]
    size = ins[0].shape[0] // 2
    copies = []
    for block in range(2):
        for i, ref in enumerate(ins):
            core = (lax.axis_index("qb") % 2) ^ (i // n_qb)
            row = core * n_qb + place_of(n_qb, *plane_partners(n_qb)[i % n_qb])
            rows = pl.ds(pl.multiple_of(row * size, size), size)
            held[block, rows] = ref[block * size : (block + 1) * size]
        copies.append(pltpu.make_async_copy(held.at[block], out.at[block], sem.at[block]))
        copies[-1].start()
    for copy in copies:
        copy.wait()


def store_kernel(parts, first, second):
    n, _, slabs, r, d = parts.shape
    for a, out in enumerate((first, second)):
        flat = out.reshape(n * r * slabs, d)
        for s in range(slabs):
            flat[pl.ds(s, n * r, stride=slabs), :] = slab_of_parts(parts, a, s)


def place_kernel(n_qa, *refs):
    blocks, (*outs, held, sem) = refs[:n_qa], refs[n_qa:]
    _, rows, slabs, d = held.shape
    r = rows // n_qa
    copies = []
    for a, out in enumerate(outs):
        flat = held.at[a].reshape(rows * slabs, d)
        for k, ref in enumerate(blocks):
            start = pl.multiple_of((lax.axis_index("qa") ^ k) * (r * slabs), r * slabs)
            for s in range(slabs):
                flat[pl.ds(start + s, r, stride=slabs), :] = ref[a, s]
        copies.append(pltpu.make_async_copy(held.at[a], out, sem.at[a]))
        copies[-1].start()
    for copy in copies:
        copy.wait()


def call(kernel, out_shape, inputs, scratch=(), flops=0, far=(), far_out=(), ride=()):
    def spec(i, x):
        near = pltpu.SMEM if x.dtype == jnp.int32 else pltpu.VMEM
        return pl.BlockSpec(memory_space=pl.ANY if i in far else near)

    outs, tree = jax.tree.flatten(out_shape)
    n_in, n_out, n_ride = len(inputs), len(outs), len(ride)
    passing = [pl.BlockSpec(memory_space=pl.ANY)] * n_ride

    def body(*refs):
        rest = refs[n_in + n_ride :]
        kernel(*refs[:n_in], *rest[:n_out], *rest[n_out + n_ride :])

    size = sum(x.size * 4 for x in inputs) + sum(x.size * 4 for x in outs)
    got = pl.pallas_call(
        body,
        out_shape=outs + [shape(*x.shape) for x in ride],
        in_specs=[spec(i, x) for i, x in enumerate(inputs)] + passing,
        out_specs=[pl.BlockSpec(memory_space=pltpu.HBM if i in far_out else pltpu.VMEM) for i in range(n_out)] + passing,
        scratch_shapes=list(scratch),
        input_output_aliases={n_in + i: n_out + i for i in range(n_ride)},
        compiler_params=pltpu.CompilerParams(vmem_limit_bytes=VMEM_LIMIT),
        cost_estimate=pl.CostEstimate(flops=flops, bytes_accessed=size, transcendentals=0),
    )(*inputs, *ride)
    result = jax.tree.unflatten(tree, got[:n_out])
    return (result, list(got[n_out:])) if n_ride else result


def shape(*dims):
    return jax.ShapeDtypeStruct(dims, F32)


def exchange(x, da, db):
    n_qa, n_qb = lax.axis_size("qa"), lax.axis_size("qb")
    pairs = [(a * n_qb + b, (a ^ da) * n_qb + (b ^ db)) for a in range(n_qa) for b in range(n_qb)]
    return lax.ppermute(x, ("qa", "qb"), pairs)


def summed(grads0, grads1):
    both = jnp.stack([grads0, grads1])
    shares = both.reshape(lax.axis_size("qa") * lax.axis_size("qb"), -1, both.shape[-1])
    share = lax.all_to_all(shares, ("qa", "qb"), 0, 0, tiled=True).sum(0, keepdims=True)
    return lax.all_to_all(jnp.broadcast_to(share, shares.shape), ("qa", "qb"), 0, 0, tiled=True)


def nothing(*refs):
    pass


def windows(n_qa):
    ks = sorted(range(1, n_qa), reverse=True)
    stages = WINDOWS
    return {k: stages[min(i, len(stages) - 1)] for i, k in enumerate(ks)}


def shards(state, costate, gates, targets):
    layout = state.shape
    rows, slabs, d = layout[2:]
    n_qa, n_qb = lax.axis_size("qa"), lax.axis_size("qb")
    scale = (n_qa * n_qb * rows * slabs) ** -0.5
    native = shape(*layout[2:])
    natives = [state.reshape(native.shape), costate.reshape(native.shape)]
    r = rows // n_qb
    parts_qa = shape(n_qa, 2, slabs, rows // n_qa, d)
    count = gates.shape[1]
    held, inner = pltpu.VMEM((2, slabs, rows, 2 * d), BF16), pltpu.VMEM((count, d, d), F32)
    def factors(blocks):
        return [(blocks, count, 2 * d, 2 * d), (blocks, count + 1, 2 * d, 2 * d)]

    products0 = shape(count, d, d)
    chain = [pltpu.VMEM(x, BF16) for x in factors(2)] + [pltpu.VMEM((4, d, d), F32)]
    work = 2 * 2 * 2 * 4 * rows * slabs * d * d
    every = count * d

    if every % (16 * n_qb) or r % 16 or n_qa % 2 or n_qb % 2:
        parts_qb = shape(n_qb, 2, slabs, r, d)
        sent = call(functools.partial(apply_kernel, 1, True), parts_qb, [targets, gates, *natives], flops=work)
        parts = lax.all_to_all(sent, "qb", 0, 0, tiled=True)
        grads1, products = call(
            functools.partial(gradient_kernel, 1, scale),
            [shape(count, d, d), products0], [targets, gates, *natives], [held, inner, *chain], 8 * work,
        )
        sent = call(functools.partial(apply_kernel, 0, False), parts_qa, [targets, gates, parts], flops=work)
        last = lax.all_to_all(sent, "qa", 0, 0, tiled=True)
        first, second = call(store_kernel, (native, native), [last])
        grads0 = call(
            functools.partial(slabs_gradient_kernel, 0, scale),
            shape(count, d, d), [targets, products, parts], [held, inner, *(pltpu.VMEM(x, BF16) for x in factors(1))], 8 * work,
        )
        whole = summed(grads0, grads1)
    else:
        blocks = call(
            functools.partial(first_kernel, 1, n_qb),
            [shape(2, slabs, r, d)] * n_qb,
            [pltpu.with_memory_space_constraint(x, pltpu.HBM) for x in (targets, gates, *natives)],
            [
                pltpu.SMEM(targets.shape, jnp.int32),
                pltpu.VMEM((1, *gates.shape[1:]), F32),
                pltpu.VMEM(native.shape, F32),
                pltpu.VMEM(native.shape, F32),
                pltpu.VMEM((d, d), F32),
                pltpu.SemaphoreType.DMA((4,)),
            ],
            work,
            far=(0, 1, 2, 3),
        )
        blocks = blocks[:1] + [exchange(x, 0, k) for k, x in enumerate(blocks) if k]
        half = shape(every // 2, d)
        square = jax.ShapeDtypeStruct((2 * d, 2 * d), BF16)
        keep1, send1, right0, left0, low, mid = call(
            functools.partial(first_gradient_kernel, 1, scale),
            [half, half, *(jax.ShapeDtypeStruct(x, BF16) for x in factors(1)), square, square],
            [targets, gates, *natives],
            [held, inner, *chain, inner, inner],
            10 * work,
        )
        got1 = exchange(send1, 0, 1)
        keep0, send0 = call(
            functools.partial(second_kernel, 0, n_qb, scale),
            [half, half],
            [targets, right0, left0, *blocks],
            [held, inner, inner],
            K0COST * work,
        )
        got0 = exchange(send0, 0, 1)
        moved, _ = call(
            functools.partial(end_kernel, n_qb),
            [shape(2, slabs, rows // n_qa, d)] * n_qa,
            [low, mid, *blocks],
            [pltpu.VMEM((2, slabs, rows, d), F32)],
            3 * work,
            ride=[keep0],
        )
        came = {0: moved[0]}
        moved = dict(enumerate(moved))
        window = windows(n_qa)

        def after(stage, kernel, out_shape, inputs, scratch=(), far=()):
            due = [k for k in window if window[k][1] == stage]
            opens = [k for k in window if window[k][0] == stage]
            ride = [came[k] for k in due] + [moved[k] for k in opens]
            if not ride:
                return call(kernel, out_shape, inputs, scratch, far=far) if out_shape else None
            result, rode = call(kernel, out_shape, inputs, scratch, far=far, ride=ride)
            came.update(zip(due, rode))
            moved.update(zip(opens, rode[len(due) :]))
            start(stage)
            return result

        def start(stage):
            for k in window:
                if window[k][0] == stage:
                    came[k] = exchange(moved[k], k, 0)

        start(0)
        partners = plane_partners(n_qb)
        size = every // n_qb
        pieces = after(
            1,
            functools.partial(spread_kernel, n_qb),
            [shape(size, d)] * n_qb,
            [keep0, got0, keep1, got1],
            [pltpu.VMEM((2, every // 2, d), F32)],
        )
        pieces = pieces[:1] + [exchange(x, dx, 2 * dy) for x, (dx, dy) in zip(pieces[1:], partners[1:])]
        mine = after("plane", plane_sum_kernel, shape(size, d), pieces)
        for i in range(1, n_qa.bit_length() - 1):
            got = exchange(mine, 1 << i, 0)
            mine = after(("line", i), sum_kernel, shape(*mine.shape), [mine, got])
        found = [mine] + [exchange(mine, dx, 2 * dy) for dx, dy in partners[1:]]
        after(("back", 0), nothing, [], [found[1]], far=(0,))
        after(("back", 1), nothing, [], [found[-1]], far=(0,))
        found = found + [exchange(x, 0, 1) for x in found]
        whole = call(
            functools.partial(collect_kernel, n_qb),
            shape(gates.shape[0], every, d),
            found,
            [pltpu.VMEM((gates.shape[0], every, d), F32), pltpu.SemaphoreType.DMA((2,))],
            far_out=(0,),
        )
        first, second = call(
            functools.partial(place_kernel, n_qa),
            (native, native),
            [came[k] for k in range(n_qa)],
            [pltpu.VMEM((2, *native.shape), F32), pltpu.SemaphoreType.DMA((2,))],
            far_out=(0, 1),
        )
    return first.reshape(layout), second.reshape(layout), whole.reshape(gates.shape)


def solution(mesh):
    in_specs = (P("qa", "qb", None, None, None), P("qa", "qb", None, None, None), P(), P())
    out_specs = (P("qa", "qb", None, None, None), P("qa", "qb", None, None, None), P())
    return jax.shard_map(shards, mesh=mesh, in_specs=in_specs, out_specs=out_specs, check_vma=False)
```
